32 devices in a mesh: fsdp: 4 (over y, x), ctx: 2 (over core), tp: 4 (over z).
Axes of the slice: x: 2, y: 2, z: 4, core: 2. Of those that a mesh axis runs over, the one named last changes fastest.
Arguments:
- inputs: bfloat16 [4, 1500, 1280], P('fsdp', 'ctx'), may hold values from -6 to 6
- lengths: int32 [4], P('fsdp'), may hold values from 375 to 1500, as said below
- cotangent: bfloat16 [4, 1500, 1280], P('fsdp', 'ctx'), may hold values from -6 to 6
- norm_gains: float32 [2, 2, 1280], replicated, may hold values from 0.5 to 1.5
- norm_shifts: float32 [2, 2, 1280], replicated, may hold values from -1 to 1
- qkv_weight: bfloat16 [2, 1280, 3, 1280], P(None, 'fsdp', None, 'tp'), may hold values from -0.15625 to 0.15625
- qv_bias: float32 [2, 2, 1280], P(None, None, 'tp'), may hold values from -1.5 to 1.5
- out_weight: bfloat16 [2, 1280, 1280], P(None, 'fsdp', 'tp'), may hold values from -0.625 to 0.625
- out_bias: float32 [2, 1280], replicated, may hold values from -1.5 to 1.5
- up_weight: bfloat16 [2, 1280, 5120], P(None, 'fsdp', 'tp'), may hold values from -0.15625 to 0.15625
- up_bias: float32 [2, 5120], P(None, 'tp'), may hold values from -1.5 to 1.5
- down_weight: bfloat16 [2, 1280, 5120], P(None, 'fsdp', 'tp'), may hold values from -0.125 to 0.125
- down_bias: float32 [2, 1280], replicated, may hold values from -1.5 to 1.5
Outputs:
- outputs: bfloat16 [4, 1500, 1280], P('fsdp', 'ctx')
- input_grad: float32 [4, 1500, 1280], P('fsdp', 'ctx')
- grad_norm_gains: float32 [2, 2, 1280], replicated
- grad_norm_shifts: float32 [2, 2, 1280], replicated
- grad_qkv: float32 [2, 1280, 3, 1280], P(None, 'fsdp', None, 'tp')
- grad_qv_bias: float32 [2, 2, 1280], P(None, None, 'tp')
- grad_out_weight: float32 [2, 1280, 1280], P(None, 'fsdp', 'tp')
- grad_out_bias: float32 [2, 1280], replicated
- grad_up_weight: float32 [2, 1280, 5120], P(None, 'fsdp', 'tp')
- grad_up_bias: float32 [2, 5120], P(None, 'tp')
- grad_down_weight: float32 [2, 1280, 5120], P(None, 'fsdp', 'tp')
- grad_down_bias: float32 [2, 1280], replicated
The draws below stay inside these ranges and needn't reach their ends.
Inputs may be any that keep to these rules, and one draw needn't show every extreme that they name: `lengths`: every clip has a length over 750, and some clip has length exactly 1500.
All inputs are finite; a program needn't handle non-finite values.
Results may differ from the reference program's by a relative error of at most 0.018.
Values may be sent and summed in bfloat16 or wider, within the bound.
No kernel may reach another device: no remote copies, remote signals or barrier semaphores. Data moves between devices by JAX's collectives and lax.ppermute only.
A program may use at most 256 MiB of HBM per device.

```python
import jax
import jax.numpy as jnp
from jax import lax

D = 1280
HEADS = 16
HEAD_DIM = 80
FF = 5120
LAYERS = 2
SLOT = 1500
CLIP_GRP = 1
CLIPS = 4


def draw_lengths(key, part):
    key = jax.random.fold_in(key, 7)
    first_key, pick_key, long_key, full_key = jax.random.split(key, 4)
    groups = CLIPS // CLIP_GRP
    base = jax.random.randint(first_key, (CLIPS,), SLOT // 4, SLOT + 1)
    picked = jax.random.randint(pick_key, (groups,), 0, CLIP_GRP)
    longer = jax.random.randint(long_key, (groups,), SLOT // 2 + 1, SLOT + 1)
    index = jnp.arange(CLIPS)
    group = index // CLIP_GRP
    chosen = index % CLIP_GRP == picked[group]
    result = jnp.where(chosen, longer[group], base)
    full_clip = jax.random.randint(full_key, (), 0, CLIPS)
    return jnp.where(index == full_clip, SLOT, result).astype(jnp.int32)


def shard_levels(rng, dims, pieces, low, largest):
    level, own = 1.0, jax.random.fold_in(rng, 6)
    for dim, blocks in pieces:
        heights = jnp.exp(jax.random.uniform(jax.random.fold_in(own, dim), (blocks,), jnp.float32, low / len(pieces), largest / len(pieces)))
        level = level * jnp.repeat(heights, dims[dim] // blocks).reshape([-1 if axis == dim else 1 for axis in range(len(dims))])
    return level


def noise(rng, dims, scale, reach, cuts=(), dtype=jnp.bfloat16):
    level = shard_levels(rng, dims, cuts, -0.22, 0.18) if cuts else 1.0
    values = jax.random.normal(rng, dims, jnp.float32) * scale * level
    return jnp.minimum(jnp.maximum(values, -reach), reach).astype(dtype)


def setup_inputs(seed: int = 0) -> dict:
    seeds = jax.random.split(jax.random.key(seed), 14)
    return {
        "inputs": noise(seeds[0], (CLIPS, SLOT, D), 1.0, 6.0, ((0, 4), (1, 2))),
        "lengths": draw_lengths(jax.random.fold_in(seeds[13], 71), 0),
        "cotangent": noise(seeds[2], (CLIPS, SLOT, D), 1.0, 6.0, ((0, 4), (1, 2))),
        "norm_gains": jnp.clip(1.0 + 0.1 * jax.random.normal(seeds[3], (LAYERS, 2, D), jnp.float32), 0.5, 1.5),
        "norm_shifts": noise(seeds[4], (LAYERS, 2, D), 0.2, 1.0, (), jnp.float32),
        "qkv_weight": noise(seeds[5], (LAYERS, D, 3, D), D ** -0.5, 0.15625, ((1, 4), (3, 4))),
        "qv_bias": noise(seeds[6], (LAYERS, 2, D), 0.3, 1.5, ((2, 4),), jnp.float32),
        "out_weight": noise(seeds[7], (LAYERS, D, D), (D // 16) ** -0.5, 0.625, ((1, 4), (2, 4))),
        "out_bias": noise(seeds[8], (LAYERS, D), 0.3, 1.5, (), jnp.float32),
        "up_weight": noise(seeds[9], (LAYERS, D, FF), D ** -0.5, 0.15625, ((1, 4), (2, 4))),
        "up_bias": noise(seeds[10], (LAYERS, FF), 0.3, 1.5, ((1, 4),), jnp.float32),
        "down_weight": noise(seeds[11], (LAYERS, D, FF), (FF // 2) ** -0.5, 0.125, ((1, 4), (2, 4))),
        "down_bias": noise(seeds[12], (LAYERS, D), 0.3, 1.5, (), jnp.float32),
    }


@jax.custom_vjp
def low(v):
    return lax.optimization_barrier(v.astype(jnp.bfloat16)).astype(jnp.float32)

@jax.custom_vjp
def low_back(v):
    return v

def low_keep(v):
    return (low(v), None)

def low_pass(kept, grad):
    return (grad,)

def back_keep(v):
    return (v, None)

def back_low(kept, grad):
    return (low(grad),)
low.defvjp(low_keep, low_pass)
low_back.defvjp(back_keep, back_low)
epsilon = 1e-05
highest = lax.Precision.HIGHEST

def normalize(rows, gain, shift):
    center = lax.optimization_barrier(jnp.mean(rows, axis=-1, keepdims=True))
    centred = rows - center
    spread = lax.optimization_barrier(jnp.mean(centred * centred, axis=-1, keepdims=True))
    return centred * lax.rsqrt(spread + epsilon) * gain + shift

def attend_clip(queries, keys, values, length):
    raw = jnp.einsum('she,the->hst', queries, keys, precision=highest) * HEAD_DIM ** (-0.5)
    scores = low_back(raw)
    valid = jnp.arange(keys.shape[0]) < length
    scores = jnp.where(valid[None, None, :], scores, -1e+30)
    top = lax.optimization_barrier(jnp.max(scores, axis=-1, keepdims=True))
    expon = jnp.exp(scores - top)
    probs = low(expon / lax.optimization_barrier(jnp.sum(expon, axis=-1, keepdims=True)))
    return jnp.einsum('hst,the->she', probs, values, precision=highest)

def forward(inputs, norm_gains, norm_shifts, qkv_weight, qv_bias, out_weight, out_bias, up_weight, up_bias, down_weight, down_bias, lengths):
    hidden = inputs
    shape = (CLIPS, SLOT, HEADS, HEAD_DIM)
    attend = jax.checkpoint(attend_clip)
    for layer in range(LAYERS):
        normed = low(normalize(hidden, norm_gains[layer, 0], norm_shifts[layer, 0]))
        mixed = jnp.einsum('csd,dte->tcse', normed, qkv_weight[layer], precision=highest)
        queries = low(low_back(mixed[0] + qv_bias[layer, 0]))
        keys = low(low_back(mixed[1]))
        values = low(low_back(mixed[2] + qv_bias[layer, 1]))
        attended = lax.map(lambda items: attend(*items), (queries.reshape(shape), keys.reshape(shape), values.reshape(shape), lengths))
        attended = low(low_back(attended.reshape(CLIPS, SLOT, D)))
        branch = low_back(jnp.einsum('cse,de->csd', attended, out_weight[layer], precision=highest))
        hidden = hidden + branch + out_bias[layer]
        normed = low(normalize(hidden, norm_gains[layer, 1], norm_shifts[layer, 1]))
        upper = low_back(jnp.einsum('csd,df->csf', normed, up_weight[layer], precision=highest) + up_bias[layer])
        active = low(jax.nn.gelu(upper, approximate=False))
        branch = low_back(jnp.einsum('csf,df->csd', active, down_weight[layer], precision=highest))
        hidden = hidden + branch + down_bias[layer]
    return hidden

def reference(inputs, lengths, cotangent, norm_gains, norm_shifts, qkv_weight, qv_bias, out_weight, out_bias, up_weight, up_bias, down_weight, down_bias):
    floats = (inputs.astype(jnp.float32), norm_gains, norm_shifts, qkv_weight.astype(jnp.float32), qv_bias, out_weight.astype(jnp.float32), out_bias, up_weight.astype(jnp.float32), up_bias, down_weight.astype(jnp.float32), down_bias)
    result, pullback = jax.vjp(lambda *values: forward(*values, lengths), *floats)
    live = (jnp.arange(SLOT)[None, :] < lengths[:, None]).astype(jnp.float32)
    grads = pullback(cotangent.astype(jnp.float32) * live[:, :, None])
    return (result.astype(jnp.bfloat16), grads[0], grads[1], grads[2], grads[3], grads[4], grads[5], grads[6], grads[7], grads[8], grads[9], grads[10])
```

```python
import functools

import jax
import jax.numpy as jnp
import numpy as np
from jax import lax
from jax.experimental import pallas as pl
from jax.experimental.pallas import tpu as pltpu
from jax.sharding import PartitionSpec as P

HEAD_DIM = 80
LANES = 128
EPSILON = 1e-05
NEG = -1e30
CHUNKS = 3
SCALE = HEAD_DIM**-0.5
SCALE2 = SCALE * float(np.log2(np.e))
BF = jnp.bfloat16
F32 = jnp.float32
NT = (((1,), (1,)), ((), ()))
NN = (((1,), (0,)), ((), ()))


def mm(a, b, dims=NN):
    return lax.dot_general(a, b, dims, preferred_element_type=F32)


def lane_iota(shape):
    return lax.broadcasted_iota(jnp.int32, shape, 1)


def split3(v):
    hi = v.astype(BF).astype(F32)
    mid = (v - hi).astype(BF).astype(F32)
    return hi, mid, v - hi - mid


def attn_fwd_kernel(q_ref, k0_ref, v0_ref, k1_ref, v1_ref, o_ref, qa_ref):
    q = q_ref[...]
    s0 = mm(q, k0_ref[0], NT)
    s1 = mm(q, k1_ref[0], NT)
    top = jnp.maximum(jnp.max(s0, axis=1, keepdims=True), jnp.max(s1, axis=1, keepdims=True))
    p0 = jnp.exp2((s0 - top) * SCALE2).astype(BF)
    p1 = jnp.exp2((s1 - top) * SCALE2).astype(BF)
    o = mm(p0, v0_ref[0]) + mm(p1, v1_ref[0])
    lane = lane_iota(o.shape)
    total = jnp.sum(jnp.where(lane == HEAD_DIM, o, 0.0), axis=1, keepdims=True)
    o_ref[...] = jnp.where(lane < HEAD_DIM, o / total, 0.0).astype(BF)
    lse = top + jnp.log2(total) * (1.0 / SCALE2)
    hi, mid, lo = split3(-lse)
    qa = jnp.where(lane == HEAD_DIM + 1, hi, q.astype(F32))
    qa = jnp.where(lane == HEAD_DIM + 2, mid, qa)
    qa = jnp.where(lane == HEAD_DIM + 3, lo, qa)
    qa_ref[...] = qa.astype(BF)


def attn_fwd(q, kv0, kv1):
    rows, width = q.shape
    span = kv0.shape[1]
    heads = width // LANES
    qspec = pl.BlockSpec((rows, LANES), lambda h: (0, h))
    kspec = pl.BlockSpec((1, span, LANES), lambda h: (0, 0, h))
    vspec = pl.BlockSpec((1, span, LANES), lambda h: (1, 0, h))
    return pl.pallas_call(
        attn_fwd_kernel,
        grid=(heads,),
        in_specs=[qspec, kspec, vspec, kspec, vspec],
        out_specs=[qspec, qspec],
        out_shape=[jax.ShapeDtypeStruct((rows, width), BF)] * 2,
        compiler_params=pltpu.CompilerParams(vmem_limit_bytes=32 * 1024 * 1024),
        cost_estimate=pl.CostEstimate(
            flops=8 * rows * span * width, bytes_accessed=8 * span * width, transcendentals=2 * rows * span * heads
        ),
        name="attn_fwd",
    )(q, kv0, kv0, kv1, kv1)


def attn_bwd_kernel(first, qa_ref, o_ref, do_ref, k0_ref, v0_ref, k1_ref, v1_ref, *refs):
    if first:
        dq_ref, dk0_ref, dv0_ref, dk1_ref, dv1_ref = refs
        olds = (None,) * 4
    else:
        olds = refs[:4]
        dq_ref, dk0_ref, dv0_ref, dk1_ref, dv1_ref = refs[4:]
    qa = qa_ref[...]
    o = o_ref[...].astype(F32)
    do = do_ref[...].astype(F32)
    lane = lane_iota(do.shape)
    delta = -jnp.sum(o * do, axis=1, keepdims=True)
    hi = delta.astype(BF).astype(F32)
    doa = jnp.where(lane == HEAD_DIM, hi, do)
    doa = jnp.where(lane == HEAD_DIM + 1, delta - hi, doa).astype(BF)
    dqt = None
    for k_ref, v_ref, dk_ref, dv_ref, dk_old, dv_old in (
        (k0_ref, v0_ref, dk0_ref, dv0_ref, olds[0], olds[1]),
        (k1_ref, v1_ref, dk1_ref, dv1_ref, olds[2], olds[3]),
    ):
        k = k_ref[0]
        st = mm(k, qa, NT)
        pt = jnp.exp2(st * SCALE2)
        dpt = mm(v_ref[0], doa, NT)
        dst = (pt * dpt).astype(BF)
        dv = mm(pt.astype(BF), doa)
        dk = mm(dst, qa)
        dv_ref[...] = dv if first else dv_old[...] + dv
        dk_ref[...] = dk if first else dk_old[...] + dk
        part = mm(k.T, dst)
        dqt = part if dqt is None else dqt + part
    dq_ref[...] = (dqt.T * SCALE).astype(BF)


def attn_bwd(qa, o, do, kv0, kv1, sums):
    rows, width = qa.shape
    span = kv0.shape[1]
    heads = width // LANES
    qspec = pl.BlockSpec((rows, LANES), lambda h: (0, h))
    kspec = pl.BlockSpec((1, span, LANES), lambda h: (0, 0, h))
    vspec = pl.BlockSpec((1, span, LANES), lambda h: (1, 0, h))
    aspec = pl.BlockSpec((span, LANES), lambda h: (0, h))
    first = sums is None
    extra = () if first else tuple(sums)
    out = pl.pallas_call(
        functools.partial(attn_bwd_kernel, first),
        grid=(heads,),
        in_specs=[qspec] * 3 + [kspec, vspec, kspec, vspec] + [aspec] * len(extra),
        out_specs=[qspec] + [aspec] * 4,
        out_shape=[jax.ShapeDtypeStruct((rows, width), BF)] + [jax.ShapeDtypeStruct((span, width), F32)] * 4,
        input_output_aliases={} if first else {7 + i: 1 + i for i in range(4)},
        compiler_params=pltpu.CompilerParams(vmem_limit_bytes=48 * 1024 * 1024),
        cost_estimate=pl.CostEstimate(
            flops=20 * rows * span * width, bytes_accessed=40 * span * width, transcendentals=2 * rows * span * heads
        ),
        name="attn_bwd",
    )(qa, o, do, kv0, kv0, kv1, kv1, *extra)
    return out[0], out[1:]


def swap(n, step):
    return [(i, i ^ step) for i in range(n)]


def tp_sum(part, tp):
    if tp != 4:
        return lax.psum(part, "tp")
    index = lax.axis_index("tp")
    edge = (index == 0) | (index == 3)
    pair = part + lax.ppermute(part, "tp", [(0, 1), (3, 2)])
    total = pair + lax.ppermute(pair, "tp", [(1, 2), (2, 1)])
    back = lax.ppermute(total, "tp", [(1, 0), (2, 3)])
    return jnp.where(edge, back, total)


def group_sum(v, fsdp):
    v = v + lax.ppermute(v, "ctx", swap(2, 1))
    step = 1
    while step < fsdp:
        v = v + lax.ppermute(v, "fsdp", swap(fsdp, step))
        step *= 2
    return v


def norm_stats(v):
    center = jnp.mean(v, axis=-1, keepdims=True)
    centred = v - center
    spread = jnp.mean(centred * centred, axis=-1, keepdims=True)
    r = lax.rsqrt(spread + EPSILON)
    return centred * r, r


def norm_back(v, gain, dn):
    xhat, r = norm_stats(v)
    dx = dn * gain
    back = r * (dx - jnp.mean(dx, axis=-1, keepdims=True) - xhat * jnp.mean(dx * xhat, axis=-1, keepdims=True))
    return back, jnp.sum(dn * xhat, axis=0), jnp.sum(dn, axis=0)


def gelu_pair(u):
    cdf = 0.5 * (1.0 + lax.erf(u * float(np.sqrt(0.5))))
    pdf = jnp.exp(-0.5 * u * u) * float(1.0 / np.sqrt(2 * np.pi))
    return u * cdf, cdf + u * pdf


def pad_rows(v, rows):
    return jnp.pad(v, ((0, rows - v.shape[0]), (0, 0))) if rows > v.shape[0] else v


def up_to(n, m):
    return -(-n // m) * m


def per_device(
    sizes,
    inputs,
    lengths,
    cotangent,
    norm_gains,
    norm_shifts,
    qkv_weight,
    qv_bias,
    out_weight,
    out_bias,
    up_weight,
    up_bias,
    down_weight,
    down_bias,
):
    fsdp, tp = sizes
    clips, rows, width = inputs.shape
    assert clips == 1
    local = qkv_weight.shape[-1]
    units = up_weight.shape[-1]
    heads = local // HEAD_DIM
    wide = heads * LANES
    layers = norm_gains.shape[0]
    me = lax.axis_index("ctx")
    full = up_to(rows, 16)
    span = up_to(rows, LANES)
    tile = up_to(-(-full // CHUNKS), LANES)
    cuts = [(a, min(full, a + tile)) for a in range(0, full, tile)]
    qrows = [up_to(b - a, LANES) for a, b in cuts]
    length = lengths[0]

    spread = np.zeros((local, wide), np.float32)
    for f in range(local):
        spread[f, f // HEAD_DIM * LANES + f % HEAD_DIM] = 1.0
    spread = jnp.asarray(spread, BF)
    gather = spread.T
    head_lane = np.arange(wide) % LANES
    q_extra = jnp.asarray((head_lane == HEAD_DIM)[None, :], F32)
    k_ones = jnp.asarray(((head_lane > HEAD_DIM) & (head_lane <= HEAD_DIM + 3))[None, :], F32)
    v_ones = jnp.asarray(((head_lane >= HEAD_DIM) & (head_lane <= HEAD_DIM + 1))[None, :], F32)
    row = jnp.arange(span)[:, None]
    live_key = (row < rows) & (row + me * rows < length)
    k_extra = k_ones + jnp.where(live_key, 0.0, NEG) * q_extra
    live_row = live_key[:full].astype(F32)

    half = qkv_weight.shape[1] // 2

    def mine(w):
        return lax.dynamic_slice_in_dim(w, me * half, half, axis=0)

    def fetch(w):
        return lax.all_gather(w, ("fsdp", "ctx"), axis=0, tiled=True)

    weights = []
    for layer in range(layers):
        q3 = mine(qkv_weight[layer]).reshape(half, 3 * local)
        attn = fetch(jnp.concatenate([q3, mine(out_weight[layer])], axis=1))
        weights.append((attn, fetch(mine(up_weight[layer])), fetch(mine(down_weight[layer]))))

    def pieces(v):
        v = jnp.pad(v[0].astype(F32), ((0, full - rows), (0, 0)))
        return [v[a:b] for a, b in cuts]

    hidden = pieces(inputs)
    saved = []
    for layer in range(layers):
        w_attn, w_up, w_down = weights[layer]
        w_qkv, w_out = w_attn[:, : 3 * local], w_attn[:, 3 * local :]
        qb, vb = qv_bias[layer, 0], qv_bias[layer, 1]
        bias3 = jnp.concatenate([qb, jnp.zeros_like(qb), vb])
        normed, mixed = [], []
        for h in hidden:
            xhat, _ = norm_stats(h)
            normed.append((xhat * norm_gains[layer, 0] + norm_shifts[layer, 0]).astype(BF))
            mixed.append((mm(normed[-1], w_qkv) + bias3).astype(BF))
        tall = pad_rows(jnp.concatenate(mixed), span)
        keys = (mm(tall[:, local : 2 * local], spread) + k_extra).astype(BF)
        values = (mm(tall[:, 2 * local :], spread) + v_ones).astype(BF)
        kv0 = jnp.stack([keys, values])
        kv1 = lax.ppermute(kv0, "ctx", swap(2, 1))
        out_chunks, qas, mids, normed2, actives, slopes, nexts = [], [], [], [], [], [], []
        attended = []
        for (a, b), qr, h, m in zip(cuts, qrows, hidden, mixed):
            q = (mm(pad_rows(m[:, :local], qr), spread) + q_extra).astype(BF)
            o, qa = attn_fwd(q, kv0, kv1)
            out_chunks.append(o)
            qas.append(qa)
            att = mm(o[: b - a], gather).astype(BF)
            attended.append(att)
            part = mm(att, w_out, NT).astype(BF)
            mids.append(h + tp_sum(part, tp).astype(F32) + out_bias[layer])
        for mid in mids:
            xhat, _ = norm_stats(mid)
            n2 = (xhat * norm_gains[layer, 1] + norm_shifts[layer, 1]).astype(BF)
            normed2.append(n2)
            act, slope = gelu_pair(mm(n2, w_up) + up_bias[layer])
            actives.append(act.astype(BF))
            slopes.append(slope.astype(BF))
            part = mm(actives[-1], w_down, NT).astype(BF)
            nexts.append(mid + tp_sum(part, tp).astype(F32) + down_bias[layer])
        saved.append((hidden, normed, qas, out_chunks, attended, kv0, kv1, mids, normed2, actives, slopes))
        hidden = nexts
    outputs = jnp.concatenate([h.astype(BF) for h in hidden])[None, :rows]

    grad = [g * live_row[a:b] for g, (a, b) in zip(pieces(cotangent), cuts)]
    owned, vectors = [None] * layers, [None] * layers

    def total(parts):
        return functools.reduce(jnp.add, parts)

    def col_sum(parts):
        return total([jnp.sum(p.astype(F32), axis=0) for p in parts])

    def weight_grad(left, right):
        return lax.dot_general(left, right, (((0,), (0,)), ((), ())), preferred_element_type=F32).astype(BF)

    def give(g):
        part = lax.psum_scatter(g, ("fsdp", "ctx"), scatter_dimension=0, tiled=True)
        other = lax.ppermute(part, "ctx", swap(2, 1))
        low = jnp.where(me == 0, part, other)
        high = jnp.where(me == 0, other, part)
        return jnp.concatenate([low, high]).astype(F32)

    for layer in reversed(range(layers)):
        hidden, normed, qas, out_chunks, attended, kv0, kv1, mids, normed2, actives, slopes = saved[layer]
        w_attn, w_up, w_down = weights[layer]
        w_qkv, w_out = w_attn[:, : 3 * local], w_attn[:, 3 * local :]
        down_bias_grad = col_sum(grad)
        lows = [g.astype(BF) for g in grad]
        d_upper, dn2 = [], []
        for gl, slope in zip(lows, slopes):
            d_upper.append((mm(gl, w_down) * slope.astype(F32)).astype(BF))
            dn2.append(tp_sum(mm(d_upper[-1], w_up, NT).astype(BF), tp).astype(F32))
        up_bias_grad = col_sum(d_upper)
        d_up_all, low_all = jnp.concatenate(d_upper), jnp.concatenate(lows)
        grad_down = give(weight_grad(low_all, jnp.concatenate(actives)))
        grad_up = give(weight_grad(jnp.concatenate(normed2), d_up_all))
        gains2, shifts2, mid_grad = [], [], []
        for g, d, mid in zip(grad, dn2, mids):
            back, gg, ss = norm_back(mid, norm_gains[layer, 1], d)
            gains2.append(gg)
            shifts2.append(ss)
            mid_grad.append(g + back)
        out_bias_grad = col_sum(mid_grad)
        lows = [g.astype(BF) for g in mid_grad]
        dqs, sums = [], None
        for (a, b), qr, gl, qa, o in zip(cuts, qrows, lows, qas, out_chunks):
            d_att = mm(gl, w_out).astype(BF)
            do = mm(pad_rows(d_att, qr), spread).astype(BF)
            dq, sums = attn_bwd(qa, o, do, kv0, kv1, sums)
            dqs.append(mm(dq[: b - a], gather).astype(BF))
        dk0, dv0, dk1, dv1 = sums
        theirs = jnp.stack([dk1 * SCALE, dv1]).astype(BF)
        got = lax.ppermute(theirs, "ctx", swap(2, 1)).astype(F32)
        dk = mm((dk0 * SCALE + got[0]).astype(BF), gather).astype(BF)[:full]
        dv = mm((dv0 + got[1]).astype(BF), gather).astype(BF)[:full]
        d_mixed = [jnp.concatenate([q, dk[a:b], dv[a:b]], axis=1) for q, (a, b) in zip(dqs, cuts)]
        grad_out_low = weight_grad(jnp.concatenate(lows), jnp.concatenate(attended))
        d_all = jnp.concatenate(d_mixed)
        grad_attn = give(jnp.concatenate([weight_grad(jnp.concatenate(normed), d_all), grad_out_low], axis=1))
        q_sum = jnp.sum(d_all[:, :local].astype(F32), axis=0)
        v_sum = jnp.sum(d_all[:, 2 * local :].astype(F32), axis=0)
        gains1, shifts1, grad = [], [], []
        for g, h, d in zip(mid_grad, hidden, d_mixed):
            dn = tp_sum(mm(d, w_qkv, NT).astype(BF), tp).astype(F32)
            back, gg, ss = norm_back(h, norm_gains[layer, 0], dn)
            gains1.append(gg)
            shifts1.append(ss)
            grad.append(g + back)
        grad_qkv = grad_attn[:, : 3 * local].reshape(-1, 3, local)
        owned[layer] = (grad_qkv, grad_attn[:, 3 * local :], grad_up, grad_down)
        flat = jnp.concatenate(
            [
                total(gains1),
                total(gains2),
                total(shifts1),
                total(shifts2),
                q_sum,
                v_sum,
                out_bias_grad,
                up_bias_grad,
                down_bias_grad,
            ]
        )
        size = flat.shape[0]
        flat = jnp.pad(flat, (0, up_to(size, 1024) - size)).reshape(-1, LANES)
        flat = group_sum(flat, fsdp).reshape(-1)
        ends = np.cumsum([width] * 4 + [local] * 2 + [width, units, width])[:-1]
        vectors[layer] = jnp.split(flat[:size], ends)

    def stack(group, index):
        return jnp.stack([group[layer][index] for layer in range(layers)])

    def both(index):
        return jnp.stack([jnp.stack([v[index], v[index + 1]]) for v in vectors])

    return (
        outputs,
        jnp.concatenate(grad)[None, :rows],
        both(0),
        both(2),
        stack(owned, 0),
        both(4),
        stack(owned, 1),
        stack(vectors, 6),
        stack(owned, 2),
        stack(vectors, 7),
        stack(owned, 3),
        stack(vectors, 8),
    )


def solution(mesh):
    in_specs = (
        P("fsdp", "ctx", None),
        P("fsdp"),
        P("fsdp", "ctx", None),
        P(),
        P(),
        P(None, "fsdp", None, "tp"),
        P(None, None, "tp"),
        P(None, "fsdp", "tp"),
        P(),
        P(None, "fsdp", "tp"),
        P(None, "tp"),
        P(None, "fsdp", "tp"),
        P(),
    )
    out_specs = (
        P("fsdp", "ctx", None),
        P("fsdp", "ctx", None),
        P(),
        P(),
        P(None, "fsdp", None, "tp"),
        P(None, None, "tp"),
        P(None, "fsdp", "tp"),
        P(),
        P(None, "fsdp", "tp"),
        P(None, "tp"),
        P(None, "fsdp", "tp"),
        P(),
    )
    sizes = (mesh.shape["fsdp"], mesh.shape["tp"])
    return jax.shard_map(
        functools.partial(per_device, sizes), mesh=mesh, in_specs=in_specs, out_specs=out_specs, check_vma=False
    )
```

```python
import functools

import jax
import jax.numpy as jnp
import numpy as np
from jax import lax
from jax.experimental import pallas as pl
from jax.experimental.pallas import tpu as pltpu
from jax.sharding import PartitionSpec as P

HEAD_DIM = 80
LANES = 128
CHUNK = 192
BACK = 384
EPSILON = 1e-05
NEG = -1e30
SCALE = HEAD_DIM**-0.5
SCALE2 = SCALE * float(np.log2(np.e))
BF = jnp.bfloat16
F32 = jnp.float32
NT = (((1,), (1,)), ((), ()))
NN = (((1,), (0,)), ((), ()))
MIB = 1024 * 1024
LIMIT = 20


def mm(a, b, dims=NN):
    return lax.dot_general(a, b, dims, preferred_element_type=F32)


def up_to(n, m):
    return -(-n // m) * m


def block(shape, index):
    return pl.BlockSpec(shape, lambda *grid: index)


def call(kernel, name, grid, ins, outs, scratch=(), flops=0, moved=0, limit=LIMIT):
    olds = [(n, o[0]) for n, o in enumerate(outs) if o[0] is not None]
    specs = [spec for _, spec in ins] + [pl.BlockSpec(memory_space=pl.ANY)] * len(olds)
    live = len(ins)

    def body(*refs):
        kernel(*refs[:live], *refs[live + len(olds) :])

    return pl.pallas_call(
        body,
        grid=grid,
        in_specs=specs,
        out_specs=[o[3] for o in outs],
        out_shape=[jax.ShapeDtypeStruct(o[1], o[2]) for o in outs],
        scratch_shapes=list(scratch),
        input_output_aliases={live + k: n for k, (n, _) in enumerate(olds)},
        compiler_params=pltpu.CompilerParams(vmem_limit_bytes=limit * MIB),
        cost_estimate=pl.CostEstimate(flops=int(flops), bytes_accessed=int(moved), transcendentals=0),
        name=name,
    )(*[a for a, _ in ins], *[o for _, o in olds])


def lane_iota(shape):
    return lax.broadcasted_iota(jnp.int32, shape, 1)


def norm_stats(v):
    center = jnp.mean(v, axis=-1, keepdims=True)
    centred = v - center
    spread = jnp.mean(centred * centred, axis=-1, keepdims=True)
    r = lax.rsqrt(spread + EPSILON)
    return centred * r, r


def norm_back(v, gain, dn):
    xhat, r = norm_stats(v)
    dx = dn * gain
    back = r * (dx - jnp.mean(dx, axis=-1, keepdims=True) - xhat * jnp.mean(dx * xhat, axis=-1, keepdims=True))
    return back, dn * xhat


def gelu_pair(u):
    cdf = 0.5 * (1.0 + lax.erf(u * float(np.sqrt(0.5))))
    pdf = jnp.exp(-0.5 * u * u) * float(1.0 / np.sqrt(2 * np.pi))
    return u * cdf, cdf + u * pdf


def summed(edge_ref, got_ref, part_ref):
    return jnp.where(edge_ref[0] == 1, got_ref[...], part_ref[...]).astype(F32)


def rows_sum(v):
    return jnp.sum(v, axis=0, keepdims=True)


def store_sums(ref, *values):
    ref[...] = jnp.zeros_like(ref)
    for n, v in enumerate(values):
        ref[0, n : n + 1, :] = v


def project_kernel(
    first, local, edge_ref, got_ref, part_ref, base_ref, add_ref, gain_ref, shift_ref, w_ref, bias_ref, spread_ref,
    ke_ref, qe_ref, ve_ref, h_ref, n_ref, q_ref, kv_ref,
):
    h = base_ref[...].astype(F32)
    if not first:
        h = h + summed(edge_ref, got_ref, part_ref) + add_ref[...]
    h_ref[...] = h
    xhat, _ = norm_stats(h)
    n = (xhat * gain_ref[...] + shift_ref[...]).astype(BF)
    n_ref[...] = n
    m = (mm(n, w_ref[...]) + bias_ref[...]).astype(BF)
    spread = spread_ref[...]
    q_ref[...] = (mm(m[:, local : 2 * local], spread) + qe_ref[...]).astype(BF)
    kv_ref[0] = (mm(m[:, 2 * local : 3 * local], spread) + ke_ref[...].astype(F32)).astype(BF)
    kv_ref[1] = (mm(m[:, 3 * local :], spread) + ve_ref[...]).astype(BF)


def split3(v):
    hi = v.astype(BF).astype(F32)
    mid = (v - hi).astype(BF).astype(F32)
    return hi, mid, v - hi - mid


def attend_kernel(
    heads, edge_ref, q_ref, k0_ref, v0_ref, k1_ref, v1_ref, gather_ref, w_ref, o_ref, qa_ref, att_ref, part_ref, acc_ref
):
    q = q_ref[...]
    s0 = mm(q, k0_ref[0], NT)
    s1 = mm(q, k1_ref[0], NT)
    top = jnp.maximum(jnp.max(s0, axis=1, keepdims=True), jnp.max(s1, axis=1, keepdims=True))
    p0 = jnp.exp2((s0 - top) * SCALE2).astype(BF)
    p1 = jnp.exp2((s1 - top) * SCALE2).astype(BF)
    o = mm(p0, v0_ref[0]) + mm(p1, v1_ref[0])
    lane = lane_iota(o.shape)
    total = jnp.sum(jnp.where(lane == HEAD_DIM, o, 0.0), axis=1, keepdims=True)
    o = jnp.where(lane < HEAD_DIM, o / total, 0.0).astype(BF)
    o_ref[...] = o
    hi, mid, lo = split3(-(top + jnp.log2(total) * (1.0 / SCALE2)))
    qa = jnp.where(lane == HEAD_DIM + 1, hi, q.astype(F32))
    qa = jnp.where(lane == HEAD_DIM + 2, mid, qa)
    qa = jnp.where(lane == HEAD_DIM + 3, lo, qa)
    qa_ref[...] = qa.astype(BF)
    head = pl.program_id(0)
    here = mm(o, gather_ref[...])

    @pl.when(head == 0)
    def _():
        acc_ref[...] = here

    @pl.when(head > 0)
    def _():
        acc_ref[...] += here

    @pl.when(head == heads - 1)
    def _():
        att = acc_ref[...].astype(BF)
        att_ref[...] = att
        part_ref[...] = mm(att, w_ref[...], NT).astype(BF)


def feed_kernel(
    back, tiles, edge_ref, got_ref, part_ref, h_ref, add_ref, gain_ref, shift_ref, up_ref, bias_ref, down_ref, *refs
):
    if back:
        (g_ref, mid_ref, n_ref, act_ref, low_ref, d_ref, out_ref, back_ref, sum_ref, usum_ref,
         n_s, acc_s, low_s, acc2_s) = refs
    else:
        mid_ref, n_ref, act_ref, slope_ref, out_ref, n_s, acc_s = refs
    tile = pl.program_id(0)

    @pl.when(tile == 0)
    def _():
        mid = h_ref[...] + summed(edge_ref, got_ref, part_ref) + add_ref[...]
        mid_ref[...] = mid
        xhat, _ = norm_stats(mid)
        n = (xhat * gain_ref[...] + shift_ref[...]).astype(BF)
        n_ref[...] = n
        n_s[...] = n
        if back:
            g = g_ref[...]
            low = g.astype(BF)
            low_ref[...] = low
            low_s[...] = low
            store_sums(sum_ref, rows_sum(g))

    act, slope = gelu_pair(mm(n_s[...], up_ref[...]) + bias_ref[...])
    act = act.astype(BF)
    act_ref[...] = act
    here = mm(act, down_ref[...], NT)
    if back:
        d = (mm(low_s[...], down_ref[...]) * slope).astype(BF)
        d_ref[...] = d
        usum_ref[...] = jnp.broadcast_to(rows_sum(d.astype(F32))[None], usum_ref.shape)
        here2 = mm(d, up_ref[...], NT)
    else:
        slope_ref[...] = slope.astype(BF)

    @pl.when(tile == 0)
    def _():
        acc_s[...] = here
        if back:
            acc2_s[...] = here2

    @pl.when(tile > 0)
    def _():
        acc_s[...] += here
        if back:
            acc2_s[...] += here2

    @pl.when(tile == tiles - 1)
    def _():
        out_ref[...] = acc_s[...].astype(BF)
        if back:
            back_ref[...] = acc2_s[...].astype(BF)


def norm2_back_kernel(
    edge_ref, got_ref, part_ref, g_ref, mid_ref, gain_ref, w_ref, spread_ref, mg_ref, low_ref, do_ref, sum_ref
):
    dn = summed(edge_ref, got_ref, part_ref)
    back, gg = norm_back(mid_ref[...], gain_ref[...], dn)
    mg = g_ref[...] + back
    mg_ref[...] = mg
    low = mg.astype(BF)
    low_ref[...] = low
    do_ref[...] = mm(mm(low, w_ref[...]).astype(BF), spread_ref[...]).astype(BF)
    store_sums(sum_ref, rows_sum(gg), rows_sum(dn), rows_sum(mg))


def attend_back_kernel(first, edge_ref, qa_ref, o_ref, do_ref, k0_ref, v0_ref, k1_ref, v1_ref, *refs):
    if first:
        dq_ref, dk0_ref, dv0_ref, dk1_ref, dv1_ref = refs
        olds = (None,) * 4
    else:
        olds = refs[:4]
        dq_ref, dk0_ref, dv0_ref, dk1_ref, dv1_ref = refs[4:]
    qa = qa_ref[...]
    do = do_ref[...].astype(F32)
    lane = lane_iota(do.shape)
    delta = -jnp.sum(o_ref[...].astype(F32) * do, axis=1, keepdims=True)
    hi = delta.astype(BF).astype(F32)
    doa = jnp.where(lane == HEAD_DIM, hi, do)
    doa = jnp.where(lane == HEAD_DIM + 1, delta - hi, doa).astype(BF)
    dqt = None
    for k_ref, v_ref, dk_ref, dv_ref, dk_old, dv_old in (
        (k0_ref, v0_ref, dk0_ref, dv0_ref, olds[0], olds[1]),
        (k1_ref, v1_ref, dk1_ref, dv1_ref, olds[2], olds[3]),
    ):
        k = k_ref[0]
        pt = jnp.exp2(mm(k, qa, NT) * SCALE2)
        dst = (pt * mm(v_ref[0], doa, NT)).astype(BF)
        dv = mm(pt.astype(BF), doa)
        dk = mm(dst, qa)
        dv_ref[...] = dv if first else dv_old[...] + dv
        dk_ref[...] = dk if first else dk_old[...] + dk
        part = mm(k.T, dst)
        dqt = part if dqt is None else dqt + part
    dq_ref[...] = (dqt.T * SCALE).astype(BF)


def project_back_kernel(
    local, edge_ref, dq_ref, dk_ref, dv_ref, got_ref, gather_ref, w_ref, d_ref, part_ref, sum_ref
):
    gather = gather_ref[...]
    dq = mm(dq_ref[...], gather).astype(BF)
    dk = mm((dk_ref[...] * SCALE + got_ref[0].astype(F32)).astype(BF), gather).astype(BF)
    dv = mm((dv_ref[...] + got_ref[1].astype(F32)).astype(BF), gather).astype(BF)
    d = jnp.concatenate([jnp.zeros_like(dq), dq, dk, dv], axis=1)
    d_ref[...] = d
    part_ref[...] = mm(d, w_ref[...], NT).astype(BF)
    store_sums(sum_ref, rows_sum(d.astype(F32)))


def norm1_back_kernel(edge_ref, got_ref, part_ref, mg_ref, h_ref, gain_ref, g_ref, sum_ref):
    dn = summed(edge_ref, got_ref, part_ref)
    back, gg = norm_back(h_ref[...], gain_ref[...], dn)
    g_ref[...] = mg_ref[...] + back
    store_sums(sum_ref, rows_sum(gg), rows_sum(dn))


def feed_back_kernel(
    tiles, edge_ref, got_ref, part_ref, mg_ref, h_ref, gain_ref, down_ref, up_ref, slope_ref,
    g_ref, low_ref, d_ref, out_ref, sum_ref, usum_ref, low_s, acc_s,
):
    tile = pl.program_id(0)

    @pl.when(tile == 0)
    def _():
        dn = summed(edge_ref, got_ref, part_ref)
        back, gg = norm_back(h_ref[...], gain_ref[...], dn)
        g = mg_ref[...] + back
        g_ref[...] = g
        low = g.astype(BF)
        low_ref[...] = low
        low_s[...] = low
        store_sums(sum_ref, rows_sum(gg), rows_sum(dn), rows_sum(g))

    d = (mm(low_s[...], down_ref[...]) * slope_ref[...].astype(F32)).astype(BF)
    d_ref[...] = d
    usum_ref[...] = jnp.broadcast_to(rows_sum(d.astype(F32))[None], usum_ref.shape)
    here = mm(d, up_ref[...], NT)

    @pl.when(tile == 0)
    def _():
        acc_s[...] = here

    @pl.when(tile > 0)
    def _():
        acc_s[...] += here

    @pl.when(tile == tiles - 1)
    def _():
        out_ref[...] = acc_s[...].astype(BF)


def swap(n, step):
    return [(i, i ^ step) for i in range(n)]


def turn_kernel(edge_ref, *refs):
    part, got, pair, there, fresh = refs[:5]
    outs = refs[5:]
    if part is not None:
        outs[0][...] = part[...] + got[...]
    if pair is not None:
        total = pair[...] + there[...]
        outs[-1][...] = total if fresh is None else jnp.where(edge_ref[0] == 1, fresh[...], total)


class Flow:
    def __init__(self, tp):
        self.tp, self.token = tp, None
        self.inward = self.across = self.outward = None
        index = lax.axis_index("tp")
        self.edge = jnp.where((index == 0) | (index == 3), 1, 0).astype(jnp.int32)[None]

    def enter(self, value):
        if self.token is not None:
            value, self.token = lax.optimization_barrier((value, self.token))
        return value

    def leave(self, value):
        self.token = value

    def knob(self):
        return self.enter(self.edge)

    def tick(self, fresh=None):
        if self.tp != 4:
            whole = lax.psum(fresh, "tp")
            return {"part": whole, "got": whole, "done": True}
        inward, across, outward = self.inward, self.across, self.outward
        got = self.got if inward or outward else None
        if outward:
            outward.update(got=got, done=True)
        job = {"part": fresh, "done": False} if fresh is not None else None
        pair = send = None
        if inward or across:
            values = [inward and inward["part"], inward and got, across and across["part"], across and self.there,
                      fresh if across else None]
            shape = (inward or across)["part"].shape
            spec = pl.BlockSpec((shape[0] // 2, shape[1]), lambda i: (i, 0))
            given = [n for n, v in enumerate(values) if v is not None]
            made = (inward is not None) + (across is not None)

            def body(edge_ref, *refs):
                full = [None] * 5
                for n, ref in zip(given, refs):
                    full[n] = ref
                turn_kernel(edge_ref, *full, *refs[len(given) :])

            res = pl.pallas_call(
                body,
                grid=(2,),
                in_specs=[pl.BlockSpec(memory_space=pltpu.SMEM)] + [spec] * len(given),
                out_specs=[spec] * made,
                out_shape=[jax.ShapeDtypeStruct(shape, BF)] * made,
                compiler_params=pltpu.CompilerParams(vmem_limit_bytes=LIMIT * MIB),
                cost_estimate=pl.CostEstimate(flops=0, bytes_accessed=14 * shape[0] * shape[1], transcendentals=0),
                name="turn",
            )(self.knob(), *[values[n] for n in given])
            self.leave(res[0])
            if inward:
                pair = res[0]
            if across:
                send = res[-1]
                across["part"] = send
        self.across = inward
        if inward:
            inward["part"] = pair
            self.there = lax.ppermute(pair, "tp", [(1, 2), (2, 1)])
        self.inward, self.outward = job, across
        if job or across:
            perm = ([(0, 1), (3, 2)] if job else []) + ([(1, 0), (2, 3)] if across else [])
            self.got = lax.ppermute(send if across else fresh, "tp", perm)
        return job

    def take(self, job):
        while not job["done"]:
            self.tick()
        return job["got"], job["part"]


def group_sum(v, fsdp):
    v = v + lax.ppermute(v, "ctx", swap(2, 1))
    step = 1
    while step < fsdp:
        v = v + lax.ppermute(v, "fsdp", swap(fsdp, step))
        step *= 2
    return v


def per_device(
    sizes,
    inputs,
    lengths,
    cotangent,
    norm_gains,
    norm_shifts,
    qkv_weight,
    qv_bias,
    out_weight,
    out_bias,
    up_weight,
    up_bias,
    down_weight,
    down_bias,
):
    fsdp, tp = sizes
    clips, rows, width = inputs.shape
    assert clips == 1
    local = qkv_weight.shape[-1]
    units = up_weight.shape[-1]
    heads = local // HEAD_DIM
    wide = heads * LANES
    square = 4 * local
    lined = up_to(local, LANES)
    layers = norm_gains.shape[0]
    last = layers - 1
    me = lax.axis_index("ctx")
    full = up_to(rows, BACK)
    count = full // CHUNK
    each = range(count)
    unit = 256 if units % 256 == 0 else LANES
    tiles = units // unit
    length = lengths[0]
    flow = Flow(tp)

    spread = np.zeros((lined, wide), np.float32)
    for f in range(local):
        spread[f, f // HEAD_DIM * LANES + f % HEAD_DIM] = 1.0
    spread_line = jnp.asarray(spread, BF)
    spread_own = jnp.asarray(spread[:local], BF)
    gather_line = jnp.asarray(spread.T, BF)
    gather_own = jnp.asarray(spread[:local].T, BF)
    head_lane = np.arange(wide) % LANES
    q_extra = jnp.asarray((head_lane == HEAD_DIM)[None, :], F32)
    k_ones = jnp.asarray(((head_lane > HEAD_DIM) & (head_lane <= HEAD_DIM + 3))[None, :], F32)
    v_ones = jnp.asarray(((head_lane >= HEAD_DIM) & (head_lane <= HEAD_DIM + 1))[None, :], F32)
    row = jnp.arange(full)[:, None]
    live = (row < rows) & (row + me * rows < length)
    k_extra = (k_ones + jnp.where(live, 0.0, NEG) * q_extra).astype(BF)

    half = qkv_weight.shape[1] // 2

    def mine(w):
        return lax.dynamic_slice_in_dim(w, me * half, half, axis=0)

    def fetch(w):
        return lax.all_gather(w, ("fsdp", "ctx"), axis=0, tiled=True)

    attn_w, up_w, down_w = [], [], []
    for layer in range(layers):
        q3 = mine(qkv_weight[layer]).reshape(half, 3 * local)
        mats = [jnp.concatenate([mine(out_weight[layer]), q3], axis=1), mine(up_weight[layer]), mine(down_weight[layer])]
        if layer == 0:
            attn = fetch(mats[0])
            feeds = fetch(jnp.concatenate(mats[1:], axis=1))
            starts = (0, 0, units)
            held = (attn, feeds, feeds)
        else:
            everything = fetch(jnp.concatenate(mats, axis=1))
            starts = (0, square, square + units)
            held = (everything,) * 3
        attn_w.append(held[0])
        up_w.append((held[1], starts[1] // unit))
        down_w.append((held[2], starts[2] // unit))

    def give(*mats):
        theirs, ours = [], []
        for g in mats:
            n = g.shape[1] // 2
            theirs.append(lax.dynamic_slice_in_dim(g, (1 - me) * n, n, axis=1))
            ours.append(lax.dynamic_slice_in_dim(g, me * n, n, axis=1))
        got = lax.ppermute(jnp.concatenate(theirs, axis=1), "ctx", swap(2, 1))
        part = lax.psum_scatter(jnp.concatenate(ours, axis=1) + got, "fsdp", scatter_dimension=0, tiled=True)
        other = lax.ppermute(part, "ctx", swap(2, 1))
        low = jnp.where(me == 0, part, other)
        high = jnp.where(me == 0, other, part)
        outs, at = [], 0
        for g in mats:
            n = g.shape[1] // 2
            outs.append(jnp.concatenate([low[:, at : at + n], high[:, at : at + n]], axis=1).astype(F32))
            at += n
        return outs

    tall = ((0, full - rows), (0, 0))
    first_input = jnp.pad(inputs[0], tall)
    first_grad = jnp.where(live, jnp.pad(cotangent[0], tall).astype(F32), 0.0)
    edge_spec = pl.BlockSpec(memory_space=pltpu.SMEM)

    def rows_of(c, cols):
        return block((CHUNK, cols), (c, 0))

    def whole(a):
        return (a, block(a.shape, (0,) * a.ndim))

    def line(v):
        return (v[None, :], block((1, v.shape[0]), (0, 0)))

    def unit_line(v):
        return (v[None, :], pl.BlockSpec((1, unit), lambda t: (0, t)))

    def unit_cols(w):
        array, first = w
        return (array, pl.BlockSpec((array.shape[0], unit), lambda t: (0, first + t)))

    sum_spec = block((1, 8, width), (0, 0, 0))
    sum_out = (None, (1, 8, width), F32, sum_spec)
    square_sum_out = (None, (1, 8, square), F32, block((1, 8, square), (0, 0, 0)))
    unit_sum_out = (None, (1, 8, units), F32, pl.BlockSpec((1, 8, unit), lambda t: (0, 0, t)))
    part_out = (None, (CHUNK, width), BF, block((CHUNK, width), (0, 0)))
    f32_rows = pltpu.VMEM((CHUNK, width), F32)
    bf_rows = pltpu.VMEM((CHUNK, width), BF)

    keep = [dict() for _ in range(layers)]
    grads = {"now": first_grad}

    def edge():
        return (flow.knob(), edge_spec)

    def both_of(job):
        spec = block((CHUNK, width), (0, 0))
        got, part = flow.take(job)
        return [(got, spec), (part, spec)]

    def out(store, name, cols, dtype, c):
        return (store.get(name) if c else None, (full, cols), dtype, rows_of(c, cols))

    def tile_out(store, name, c):
        return (store.get(name) if c else None, (full, units), BF, pl.BlockSpec((CHUNK, unit), lambda t: (c, t)))

    def project(layer, c, job):
        k = keep[layer]
        if job is None:
            pair = [(jnp.zeros((8, LANES), BF), block((8, LANES), (0, 0)))] * 2
            base, add = first_input, jnp.zeros((width,), F32)
        else:
            pair = both_of(job)
            base, add = keep[layer - 1]["mid"], down_bias[layer - 1]
        qb, vb = qv_bias[layer, 0], qv_bias[layer, 1]
        bias = jnp.concatenate([jnp.zeros_like(qb), qb, jnp.zeros_like(qb), vb])
        ins = [edge(), *pair, (base, rows_of(c, width)), line(add), line(norm_gains[layer, 0]), line(norm_shifts[layer, 0]),
               (attn_w[layer], block((width, square), (0, 0))), line(bias), whole(spread_own), (k_extra, rows_of(c, wide)), whole(q_extra), whole(v_ones)]
        outs = [out(k, "hidden", width, F32, c), out(k, "normed", width, BF, c), out(k, "q", wide, BF, c),
                (k.get("kv0") if c else None, (2, full, wide), BF, block((2, CHUNK, wide), (0, c, 0)))]
        res = call(functools.partial(project_kernel, job is None, local), "project", (1,), ins, outs,
                   flops=2 * CHUNK * width * square, moved=2 * width * square)
        k["hidden"], k["normed"], k["q"], k["kv0"] = res
        flow.leave(res[2])

    def share(layer):
        k = keep[layer]
        k["kv1"] = lax.ppermute(k["kv0"], "ctx", swap(2, 1))

    def head_specs(c, rows=CHUNK):
        q = pl.BlockSpec((rows, LANES), lambda h: (c, h))
        keys = pl.BlockSpec((1, full, LANES), lambda h: (0, 0, h))
        values = pl.BlockSpec((1, full, LANES), lambda h: (1, 0, h))
        return q, keys, values

    def attend(layer, c):
        k = keep[layer]
        q, keys, values = head_specs(c)
        ins = [edge(), (k["q"], q), (k["kv0"], keys), (k["kv0"], values), (k["kv1"], keys), (k["kv1"], values),
               (gather_line, pl.BlockSpec((LANES, lined), lambda h: (h, 0))),
               (attn_w[layer], block((width, lined), (0, 0)))]
        outs = [(k.get("o") if c else None, (full, wide), BF, q), (k.get("qa") if c else None, (full, wide), BF, q),
                out(k, "attended", lined, BF, c), part_out]
        res = call(functools.partial(attend_kernel, heads), "attend", (heads,), ins, outs,
                   [pltpu.VMEM((CHUNK, lined), F32)], flops=8 * CHUNK * full * wide, moved=8 * full * wide)
        k["o"], k["qa"], k["attended"], part = res
        flow.leave(part)
        return flow.tick(part)

    def feed(layer, c, job):
        k = keep[layer]
        back = layer == last
        pair = both_of(job)
        ins = [edge(), *pair, (k["hidden"], rows_of(c, width)), line(out_bias[layer]), line(norm_gains[layer, 1]),
               line(norm_shifts[layer, 1]), unit_cols(up_w[layer]), unit_line(up_bias[layer]), unit_cols(down_w[layer])]
        outs = [out(k, "mid", width, F32, c), out(k, "normed2", width, BF, c), tile_out(k, "active", c)]
        scratch = [bf_rows, f32_rows]
        if back:
            ins.append((grads["now"], rows_of(c, width)))
            outs += [out(k, "low", width, BF, c), tile_out(k, "d_upper", c), out(k, "late", width, BF, c), part_out,
                     sum_out, unit_sum_out]
            scratch += [bf_rows, f32_rows]
        else:
            outs += [tile_out(k, "slope", c), part_out]
        res = call(functools.partial(feed_kernel, back, tiles), "feed", (tiles,), ins, outs, scratch,
                   flops=4 * CHUNK * width * units, moved=4 * width * units)
        k["mid"], k["normed2"], k["active"] = res[:3]
        if back:
            k["low"], k["d_upper"], k["late"], part_back, s, us = res[3:]
            k.setdefault("down_b", []).append(s[0, 0])
            k.setdefault("up_b", []).append(us[0, 0])
            flow.leave(part_back)
            return flow.tick(part_back)
        k["slope"], part = res[3:]
        flow.leave(part)
        return flow.tick(part)

    def norm2_back(layer, c, job):
        k = keep[layer]
        pair = both_of(job)
        ins = [edge(), *pair, (grads["now"], rows_of(c, width)), (k["mid"], rows_of(c, width)), line(norm_gains[layer, 1]),
               (attn_w[layer], block((width, lined), (0, 0))), whole(spread_line)]
        outs = [out(k, "mid_grad", width, F32, c), out(k, "low2", width, BF, c), out(k, "do", wide, BF, c), sum_out]
        k["mid_grad"], k["low2"], k["do"], s = call(norm2_back_kernel, "norm2_back", (1,), ins, outs,
                                                    flops=2 * CHUNK * width * lined, moved=20 * CHUNK * width)
        k.setdefault("gains2", []).append(s[0, 0])
        k.setdefault("shifts2", []).append(s[0, 1])
        k.setdefault("out_b", []).append(s[0, 2])
        flow.leave(k["do"])

    def attend_back(layer, c, sums):
        k = keep[layer]
        q, keys, values = head_specs(c, BACK)
        acc = pl.BlockSpec((full, LANES), lambda h: (0, h))
        first = sums is None
        ins = [edge(), (k["qa"], q), (k["o"], q), (k["do"], q), (k["kv0"], keys), (k["kv0"], values), (k["kv1"], keys),
               (k["kv1"], values)]
        live_in = len(ins)
        olds = [] if first else [(s, acc) for s in sums]
        old_dq = k.get("dq") if c else None
        everything = ins + olds + ([] if old_dq is None else [(old_dq, pl.BlockSpec(memory_space=pl.ANY))])
        aliases = {} if first else {live_in + n: 1 + n for n in range(4)}
        if old_dq is not None:
            aliases[len(everything) - 1] = 0

        def body(*refs):
            kept = live_in + len(olds)
            attend_back_kernel(first, *refs[:kept], *refs[len(everything) :])

        res = pl.pallas_call(
            body,
            grid=(heads,),
            in_specs=[s for _, s in everything],
            out_specs=[q] + [acc] * 4,
            out_shape=[jax.ShapeDtypeStruct((full, wide), BF)] + [jax.ShapeDtypeStruct((full, wide), F32)] * 4,
            input_output_aliases=aliases,
            compiler_params=pltpu.CompilerParams(vmem_limit_bytes=LIMIT * MIB),
            cost_estimate=pl.CostEstimate(flops=20 * BACK * full * wide, bytes_accessed=40 * full * wide, transcendentals=0),
            name="attend_back",
        )(*[a for a, _ in everything])
        k["dq"] = res[0]
        flow.leave(res[0])
        return res[1:]

    def share_back(sums):
        dk0, dv0, dk1, dv1 = sums
        theirs = jnp.stack([dk1 * SCALE, dv1]).astype(BF)
        return dk0, dv0, lax.ppermute(theirs, "ctx", swap(2, 1))

    def project_back(layer, c, shared):
        k = keep[layer]
        dk0, dv0, got = shared
        ins = [edge(), (k["dq"], rows_of(c, wide)), (dk0, rows_of(c, wide)), (dv0, rows_of(c, wide)),
               (got, block((2, CHUNK, wide), (0, c, 0))), whole(gather_own), (attn_w[layer], block((width, square), (0, 0)))]
        outs = [out(k, "d_mixed", square, BF, c), part_out, square_sum_out]
        k["d_mixed"], part, s = call(functools.partial(project_back_kernel, local), "project_back", (1,), ins, outs,
                                     flops=2 * CHUNK * width * square, moved=2 * width * square)
        k.setdefault("mixed_b", []).append(s[0, 0])
        flow.leave(part)
        return flow.tick(part)

    def norm1_back(layer, c, job):
        k = keep[layer]
        pair = both_of(job)
        ins = [edge(), *pair, (k["mid_grad"], rows_of(c, width)), (k["hidden"], rows_of(c, width)), line(norm_gains[layer, 0])]
        outs = [out(k, "grad", width, F32, c), sum_out]
        k["grad"], s = call(norm1_back_kernel, "norm1_back", (1,), ins, outs, moved=20 * CHUNK * width)
        k.setdefault("gains1", []).append(s[0, 0])
        k.setdefault("shifts1", []).append(s[0, 1])
        flow.leave(k["grad"])

    def feed_back(layer, c, job):
        k, b = keep[layer], keep[layer - 1]
        pair = both_of(job)
        ins = [edge(), *pair, (k["mid_grad"], rows_of(c, width)), (k["hidden"], rows_of(c, width)), line(norm_gains[layer, 0]),
               unit_cols(down_w[layer - 1]), unit_cols(up_w[layer - 1]),
               (b["slope"], pl.BlockSpec((CHUNK, unit), lambda t: (c, t)))]
        outs = [out(k, "grad", width, F32, c), out(b, "low", width, BF, c), tile_out(b, "d_upper", c), part_out, sum_out,
                unit_sum_out]
        res = call(functools.partial(feed_back_kernel, tiles), "feed_back", (tiles,), ins, outs, [bf_rows, f32_rows],
                   flops=4 * CHUNK * width * units, moved=4 * width * units)
        k["grad"], b["low"], b["d_upper"], part, s, us = res
        k.setdefault("gains1", []).append(s[0, 0])
        k.setdefault("shifts1", []).append(s[0, 1])
        b.setdefault("down_b", []).append(s[0, 2])
        b.setdefault("up_b", []).append(us[0, 0])
        flow.leave(part)
        return flow.tick(part)

    def weight_grad(left, right):
        return lax.dot_general(left, right, (((0,), (0,)), ((), ())), preferred_element_type=F32).astype(BF)

    owned = [dict() for _ in range(layers)]

    def grad_feed(layer):
        k = keep[layer]
        down = weight_grad(flow.enter(k["low"]), k["active"])
        flow.leave(down)
        up = weight_grad(flow.enter(k["normed2"]), k["d_upper"])
        flow.leave(up)
        owned[layer]["up"], owned[layer]["down"] = give(up, down)

    def grad_attn(layer):
        k = keep[layer]
        g1 = weight_grad(flow.enter(k["normed"]), k["d_mixed"])
        g2 = weight_grad(k["low2"], k["attended"])
        g = jnp.concatenate([g2[:, :local], g1[:, local:]], axis=1)
        flow.leave(g)
        (owned[layer]["attn"],) = give(g)

    jobs = [None] * count
    for layer in range(layers):
        for c in each:
            project(layer, c, jobs[c])
        share(layer)
        jobs = [attend(layer, c) for c in each]
        jobs = [feed(layer, c, jobs[c]) for c in each]
    k = keep[last]
    final = lax.psum(k["late"], "tp").astype(F32)
    outputs = (k["mid"] + final + down_bias[last]).astype(BF)
    vectors = [None] * layers
    for layer in reversed(range(layers)):
        k = keep[layer]
        sums = None
        for c in each:
            norm2_back(layer, c, jobs[c])
            if (c + 1) * CHUNK % BACK == 0:
                sums = attend_back(layer, c * CHUNK // BACK, sums)
        shared = share_back(sums)
        grad_feed(layer)
        jobs = [project_back(layer, c, shared) for c in each]
        grad_attn(layer)
        for c in each:
            if layer > 0:
                jobs[c] = feed_back(layer, c, jobs[c])
            else:
                norm1_back(layer, c, jobs[c])
        grads["now"] = k["grad"]
        total = {n: functools.reduce(jnp.add, k[n])
                 for n in ("gains1", "gains2", "shifts1", "shifts2", "mixed_b", "out_b", "up_b", "down_b")}
        mixed = total["mixed_b"]
        flat = jnp.concatenate(
            [total["gains1"], total["gains2"], total["shifts1"], total["shifts2"], mixed[local : 2 * local],
             mixed[3 * local :], total["out_b"], total["up_b"], total["down_b"]]
        )
        size = flat.shape[0]
        flat = jnp.pad(flat, (0, up_to(size, 1024) - size)).reshape(-1, LANES)
        flat = group_sum(flat, fsdp).reshape(-1)
        ends = np.cumsum([width] * 4 + [local] * 2 + [width, units, width])[:-1]
        vectors[layer] = jnp.split(flat[:size], ends)

    def stack(index):
        return jnp.stack([v[index] for v in vectors])

    def both(index):
        return jnp.stack([jnp.stack([v[index], v[index + 1]]) for v in vectors])

    def matrices(name):
        return jnp.stack([o[name] for o in owned])

    attn = matrices("attn")
    return (
        outputs[None, :rows],
        grads["now"][None, :rows],
        both(0),
        both(2),
        attn[:, :, local:].reshape(layers, -1, 3, local),
        both(4),
        attn[:, :, :local],
        stack(6),
        matrices("up"),
        stack(7),
        matrices("down"),
        stack(8),
    )


def solution(mesh):
    in_specs = (
        P("fsdp", "ctx", None),
        P("fsdp"),
        P("fsdp", "ctx", None),
        P(),
        P(),
        P(None, "fsdp", None, "tp"),
        P(None, None, "tp"),
        P(None, "fsdp", "tp"),
        P(),
        P(None, "fsdp", "tp"),
        P(None, "tp"),
        P(None, "fsdp", "tp"),
        P(),
    )
    out_specs = (
        P("fsdp", "ctx", None),
        P("fsdp", "ctx", None),
        P(),
        P(),
        P(None, "fsdp", None, "tp"),
        P(None, None, "tp"),
        P(None, "fsdp", "tp"),
        P(),
        P(None, "fsdp", "tp"),
        P(None, "tp"),
        P(None, "fsdp", "tp"),
        P(),
    )
    sizes = (mesh.shape["fsdp"], mesh.shape["tp"])
    return jax.shard_map(
        functools.partial(per_device, sizes), mesh=mesh, in_specs=in_specs, out_specs=out_specs, check_vma=False
    )
```

```python
import functools

import jax
import jax.numpy as jnp
import numpy as np
from jax import lax
from jax.experimental import pallas as pl
from jax.experimental.layout import Layout, with_layout_constraint
from jax.experimental.pallas import tpu as pltpu
from jax.sharding import PartitionSpec as P

HEAD_DIM = 80
LANES = 128
CHUNK = 192
BACK = 384
EPSILON = 1e-05
NEG = -1e30
SCALE = HEAD_DIM**-0.5
SCALE2 = SCALE * float(np.log2(np.e))
BF = jnp.bfloat16
F32 = jnp.float32
NT = (((1,), (1,)), ((), ()))
NN = (((1,), (0,)), ((), ()))
MIB = 1024 * 1024
LIMIT = 20
COST = 0.1


def mm(a, b, dims=NN):
    return lax.dot_general(a, b, dims, preferred_element_type=F32)


def up_to(n, m):
    return -(-n // m) * m


def block(shape, index):
    return pl.BlockSpec(shape, lambda *grid: index)


def call(kernel, name, grid, ins, outs, scratch=(), flops=0, moved=0, limit=LIMIT):
    olds = [(n, o[0]) for n, o in enumerate(outs) if o[0] is not None]
    specs = [spec for _, spec in ins] + [pl.BlockSpec(memory_space=pl.ANY)] * len(olds)
    live = len(ins)

    def body(*refs):
        kernel(*refs[:live], *refs[live + len(olds) :])

    return pl.pallas_call(
        body,
        grid=grid,
        in_specs=specs,
        out_specs=[o[3] for o in outs],
        out_shape=[jax.ShapeDtypeStruct(o[1], o[2]) for o in outs],
        scratch_shapes=list(scratch),
        input_output_aliases={live + k: n for k, (n, _) in enumerate(olds)},
        compiler_params=pltpu.CompilerParams(vmem_limit_bytes=limit * MIB),
        cost_estimate=pl.CostEstimate(flops=int(flops * COST), bytes_accessed=int(moved * COST), transcendentals=0),
        name=name,
    )(*[a for a, _ in ins], *[o for _, o in olds])


def lane_iota(shape):
    return lax.broadcasted_iota(jnp.int32, shape, 1)


def norm_stats(v):
    center = jnp.mean(v, axis=-1, keepdims=True)
    centred = v - center
    spread = jnp.mean(centred * centred, axis=-1, keepdims=True)
    r = lax.rsqrt(spread + EPSILON)
    return centred * r, r


def norm_back(x_ref, r_ref, gain, dn):
    xhat, r = x_ref[...].astype(F32), r_ref[:, :1]
    dx = dn * gain
    back = r * (dx - jnp.mean(dx, axis=-1, keepdims=True) - xhat * jnp.mean(dx * xhat, axis=-1, keepdims=True))
    return back, dn * xhat


def gelu_pair(u):
    cdf = 0.5 * (1.0 + lax.erf(u * float(np.sqrt(0.5))))
    pdf = jnp.exp(-0.5 * u * u) * float(1.0 / np.sqrt(2 * np.pi))
    return u * cdf, cdf + u * pdf


def summed(edge_ref, got_ref, part_ref):
    return jnp.where(edge_ref[0] == 1, got_ref[...], part_ref[...]).astype(F32)


def rows_sum(v):
    return jnp.sum(v, axis=0, keepdims=True)


def keep_norm(xhat, r, x_ref, r_ref):
    x_ref[...] = xhat.astype(BF)
    r_ref[...] = jnp.broadcast_to(r, r_ref.shape)


def add_sums(ref, at, *values):
    for n, v in enumerate(values):
        ref[at + n : at + n + 1, : v.shape[1]] += v


NORM1_ROW, NORM2_ROW, OUT_ROW, DOWN_ROW, MIXED_ROW, UP_ROW = 0, 2, 4, 5, 6, 7


def add_unit_sums(ref, tile, d):
    n = d.shape[1]
    ref[UP_ROW : UP_ROW + 1, pl.ds(pl.multiple_of(tile * n, n), n)] += rows_sum(d.astype(F32))


def project_kernel(
    first, local, edge_ref, got_ref, part_ref, base_ref, add_ref, gain_ref, shift_ref, w_ref, bias_ref, spread_ref,
    ke_ref, qe_ref, ve_ref, h_ref, x_ref, r_ref, n_ref, q_ref, kv_ref,
):
    h = base_ref[...].astype(F32)
    if not first:
        h = h + summed(edge_ref, got_ref, part_ref) + add_ref[...]
    h_ref[...] = h
    xhat, r = norm_stats(h)
    keep_norm(xhat, r, x_ref, r_ref)
    n = (xhat * gain_ref[...] + shift_ref[...]).astype(BF)
    n_ref[...] = n
    m = (mm(n, w_ref[...]) + bias_ref[...]).astype(BF)
    spread = spread_ref[...]
    q_ref[...] = (mm(m[:, local : 2 * local], spread) + qe_ref[...]).astype(BF)
    kv_ref[0] = (mm(m[:, 2 * local : 3 * local], spread) + ke_ref[...].astype(F32)).astype(BF)
    kv_ref[1] = (mm(m[:, 3 * local :], spread) + ve_ref[...]).astype(BF)


def split3(v):
    hi = v.astype(BF).astype(F32)
    mid = (v - hi).astype(BF).astype(F32)
    return hi, mid, v - hi - mid


def attend_kernel(
    heads, edge_ref, q_ref, k0_ref, v0_ref, k1_ref, v1_ref, gather_ref, w_ref, o_ref, qa_ref, att_ref, part_ref, acc_ref
):
    q = q_ref[...]
    s0 = mm(q, k0_ref[0], NT)
    s1 = mm(q, k1_ref[0], NT)
    top = jnp.maximum(jnp.max(s0, axis=1, keepdims=True), jnp.max(s1, axis=1, keepdims=True))
    p0 = jnp.exp2((s0 - top) * SCALE2).astype(BF)
    p1 = jnp.exp2((s1 - top) * SCALE2).astype(BF)
    o = mm(p0, v0_ref[0]) + mm(p1, v1_ref[0])
    lane = lane_iota(o.shape)
    total = jnp.sum(jnp.where(lane == HEAD_DIM, o, 0.0), axis=1, keepdims=True)
    o = jnp.where(lane < HEAD_DIM, o / total, 0.0).astype(BF)
    o_ref[...] = o
    hi, mid, lo = split3(-(top + jnp.log2(total) * (1.0 / SCALE2)))
    qa = jnp.where(lane == HEAD_DIM + 1, hi, q.astype(F32))
    qa = jnp.where(lane == HEAD_DIM + 2, mid, qa)
    qa = jnp.where(lane == HEAD_DIM + 3, lo, qa)
    qa_ref[...] = qa.astype(BF)
    head = pl.program_id(0)
    here = mm(o, gather_ref[...])

    @pl.when(head == 0)
    def _():
        acc_ref[...] = here

    @pl.when(head > 0)
    def _():
        acc_ref[...] += here

    @pl.when(head == heads - 1)
    def _():
        att = acc_ref[...].astype(BF)
        att_ref[...] = att
        part_ref[...] = mm(att, w_ref[...], NT).astype(BF)


def feed_kernel(
    back, tiles, edge_ref, got_ref, part_ref, h_ref, add_ref, gain_ref, shift_ref, up_ref, bias_ref, down_ref, *refs
):
    if back:
        (g_ref, old_ref, mid_ref, x_ref, r_ref, n_ref, act_ref, low_ref, d_ref, out_ref, back_ref, sum_ref,
         n_s, acc_s, low_s, acc2_s) = refs
    else:
        mid_ref, x_ref, r_ref, n_ref, act_ref, slope_ref, out_ref, n_s, acc_s = refs
    tile = pl.program_id(0)

    @pl.when(tile == 0)
    def _():
        mid = h_ref[...] + summed(edge_ref, got_ref, part_ref) + add_ref[...]
        mid_ref[...] = mid
        xhat, r = norm_stats(mid)
        keep_norm(xhat, r, x_ref, r_ref)
        n = (xhat * gain_ref[...] + shift_ref[...]).astype(BF)
        n_ref[...] = n
        n_s[...] = n
        if back:
            low = g_ref[...]
            low_ref[...] = low
            low_s[...] = low
            sum_ref[...] = old_ref[...]
            add_sums(sum_ref, DOWN_ROW, rows_sum(low.astype(F32)))

    act, slope = gelu_pair(mm(n_s[...], up_ref[...]) + bias_ref[...])
    act = act.astype(BF)
    act_ref[...] = act
    here = mm(act, down_ref[...], NT)
    if back:
        d = (mm(low_s[...], down_ref[...]) * slope).astype(BF)
        d_ref[...] = d
        add_unit_sums(sum_ref, tile, d)
        here2 = mm(d, up_ref[...], NT)
    else:
        slope_ref[...] = slope.astype(BF)

    @pl.when(tile == 0)
    def _():
        acc_s[...] = here
        if back:
            acc2_s[...] = here2

    @pl.when(tile > 0)
    def _():
        acc_s[...] += here
        if back:
            acc2_s[...] += here2

    @pl.when(tile == tiles - 1)
    def _():
        out_ref[...] = acc_s[...].astype(BF)
        if back:
            back_ref[...] = acc2_s[...].astype(BF)


def norm2_back_kernel(
    edge_ref, got_ref, part_ref, g_ref, x_ref, r_ref, gain_ref, w_ref, spread_ref, old_ref, mg_ref, low_ref, do_ref, sum_ref
):
    dn = summed(edge_ref, got_ref, part_ref)
    back, gg = norm_back(x_ref, r_ref, gain_ref[...], dn)
    mg = g_ref[...].astype(F32) + back
    mg_ref[...] = mg
    low = mg.astype(BF)
    low_ref[...] = low
    do_ref[...] = mm(mm(low, w_ref[...]).astype(BF), spread_ref[...]).astype(BF)
    sum_ref[...] = old_ref[...]
    add_sums(sum_ref, NORM2_ROW, rows_sum(gg), rows_sum(dn), rows_sum(mg))


def attend_back_kernel(first, done, edge_ref, qa_ref, o_ref, do_ref, k0_ref, v0_ref, k1_ref, v1_ref, *refs):
    olds = (None,) * 4 if first else refs[:4]
    dq_ref, dk0_ref, dv0_ref, *rest = refs[len(refs) - (4 if done else 5) :]
    dk1_ref, dv1_ref = (None, None) if done else rest
    qa = qa_ref[...]
    do = do_ref[...].astype(F32)
    lane = lane_iota(do.shape)
    delta = -jnp.sum(o_ref[...].astype(F32) * do, axis=1, keepdims=True)
    hi = delta.astype(BF).astype(F32)
    doa = jnp.where(lane == HEAD_DIM, hi, do)
    doa = jnp.where(lane == HEAD_DIM + 1, delta - hi, doa).astype(BF)
    dqt = None
    for k_ref, v_ref, dk_ref, dv_ref, dk_old, dv_old in (
        (k0_ref, v0_ref, dk0_ref, dv0_ref, olds[0], olds[1]),
        (k1_ref, v1_ref, dk1_ref, dv1_ref, olds[2], olds[3]),
    ):
        k = k_ref[0]
        pt = jnp.exp2(mm(k, qa, NT) * SCALE2)
        dst = (pt * mm(v_ref[0], doa, NT)).astype(BF)
        dv = mm(pt.astype(BF), doa)
        dk = mm(dst, qa)
        if not first:
            dv, dk = dv_old[...] + dv, dk_old[...] + dk
        if dk_ref is None:
            rest[0][0] = (dk * SCALE).astype(BF)
            rest[0][1] = dv.astype(BF)
        else:
            dk_ref[...] = dk
            dv_ref[...] = dv
        part = mm(k.T, dst)
        dqt = part if dqt is None else dqt + part
    dq_ref[...] = (dqt.T * SCALE).astype(BF)


def project_back_kernel(
    local, edge_ref, dq_ref, dk_ref, dv_ref, got_ref, gather_ref, w_ref, old_ref, d_ref, part_ref, sum_ref
):
    gather = gather_ref[...]
    dq = mm(dq_ref[...], gather).astype(BF)
    dk = mm((dk_ref[...] * SCALE + got_ref[0].astype(F32)).astype(BF), gather).astype(BF)
    dv = mm((dv_ref[...] + got_ref[1].astype(F32)).astype(BF), gather).astype(BF)
    d = jnp.concatenate([jnp.zeros_like(dq), dq, dk, dv], axis=1)
    d_ref[...] = d
    part_ref[...] = mm(d, w_ref[...], NT).astype(BF)
    sum_ref[...] = old_ref[...]
    add_sums(sum_ref, MIXED_ROW, rows_sum(d.astype(F32)))


def norm1_back_kernel(edge_ref, got_ref, part_ref, mg_ref, x_ref, r_ref, gain_ref, old_ref, g_ref, sum_ref):
    dn = summed(edge_ref, got_ref, part_ref)
    back, gg = norm_back(x_ref, r_ref, gain_ref[...], dn)
    g_ref[...] = (mg_ref[...] + back).reshape(g_ref.shape)
    sum_ref[...] = old_ref[...]
    add_sums(sum_ref, NORM1_ROW, rows_sum(gg), rows_sum(dn))


def output_kernel(edge_ref, got_ref, part_ref, mid_ref, add_ref, out_ref):
    out_ref[...] = (mid_ref[...] + summed(edge_ref, got_ref, part_ref) + add_ref[...]).astype(BF)


def vectors_kernel(layers, local, sum_ref, gain_ref, shift_ref, qv_ref, out_ref, up_ref, down_ref):
    for n in range(layers):
        def row(at, start, size):
            return sum_ref[8 * n + at : 8 * n + at + 1, :][:, start : start + size]

        width = gain_ref.shape[2]
        for at, first in ((0, NORM1_ROW), (1, NORM2_ROW)):
            gain_ref[n, at : at + 1, :] = row(first, 0, width)
            shift_ref[n, at : at + 1, :] = row(first + 1, 0, width)
        qv_ref[n, 0:1, :] = row(MIXED_ROW, local, local)
        qv_ref[n, 1:2, :] = row(MIXED_ROW, 3 * local, local)
        out_ref[n : n + 1, :] = row(OUT_ROW, 0, width)
        up_ref[n : n + 1, :] = row(UP_ROW, 0, up_ref.shape[1])
        down_ref[n : n + 1, :] = row(DOWN_ROW, 0, width)


def finish_kernel(cuts, me_ref, own_ref, other_ref, *out_refs):
    half = own_ref.shape[2]
    first = me_ref[0] == 0
    for m in range(own_ref.shape[1]):
        for at, (a, b) in ((0, (own_ref, other_ref)), (half, (other_ref, own_ref))):
            v = jnp.where(first, a[0, m].astype(F32), b[0, m].astype(F32))
            if cuts is None:
                out_refs[m][0, at : at + half, :] = v
            else:
                out_refs[0][0, at : at + half, :] = v[:, :cuts]
                for t in range(3):
                    out_refs[1][0, t, at : at + half, :] = v[:, (t + 1) * cuts : (t + 2) * cuts]


def feed_back_kernel(
    tiles, edge_ref, got_ref, part_ref, mg_ref, x_ref, r_ref, gain_ref, down_ref, up_ref, slope_ref, old_ref, lold_ref,
    g_ref, low_ref, d_ref, out_ref, sum_ref, lsum_ref, low_s, acc_s,
):
    tile = pl.program_id(0)

    @pl.when(tile == 0)
    def _():
        dn = summed(edge_ref, got_ref, part_ref)
        back, gg = norm_back(x_ref, r_ref, gain_ref[...], dn)
        g = mg_ref[...] + back
        g_ref[...] = g
        low = g.astype(BF)
        low_ref[...] = low
        low_s[...] = low
        sum_ref[...] = old_ref[...]
        lsum_ref[...] = lold_ref[...]
        add_sums(sum_ref, NORM1_ROW, rows_sum(gg), rows_sum(dn))
        add_sums(lsum_ref, DOWN_ROW, rows_sum(g))

    d = (mm(low_s[...], down_ref[...]) * slope_ref[...].astype(F32)).astype(BF)
    d_ref[...] = d
    add_unit_sums(lsum_ref, tile, d)
    here = mm(d, up_ref[...], NT)

    @pl.when(tile == 0)
    def _():
        acc_s[...] = here

    @pl.when(tile > 0)
    def _():
        acc_s[...] += here

    @pl.when(tile == tiles - 1)
    def _():
        out_ref[...] = acc_s[...].astype(BF)


def swap(n, step):
    return [(i, i ^ step) for i in range(n)]


def turn_kernel(edge_ref, *refs):
    part, got, pair, there, fresh = refs[:5]
    outs = refs[5:]
    if part is not None:
        outs[0][...] = part[...] + got[...]
    if pair is not None:
        total = pair[...] + there[...]
        outs[-1][...] = total if fresh is None else jnp.where(edge_ref[0] == 1, fresh[...], total)


class Flow:
    def __init__(self, tp):
        self.tp, self.token = tp, None
        self.inward = self.across = self.outward = None
        index = lax.axis_index("tp")
        self.edge = jnp.where((index == 0) | (index == 3), 1, 0).astype(jnp.int32)[None]

    def enter(self, value):
        if self.token is not None:
            value, self.token = lax.optimization_barrier((value, self.token))
        return value

    def leave(self, value):
        self.token = value

    def knob(self):
        return self.enter(self.edge)

    def tick(self, fresh=None):
        if self.tp != 4:
            whole = lax.psum(fresh, "tp")
            return {"part": whole, "got": whole, "done": True}
        inward, across, outward = self.inward, self.across, self.outward
        got = self.got if inward or outward else None
        if outward:
            outward.update(got=got, done=True)
        job = {"part": fresh, "done": False} if fresh is not None else None
        pair = send = None
        if inward or across:
            values = [inward and inward["part"], inward and got, across and across["part"], across and self.there,
                      fresh if across else None]
            shape = (inward or across)["part"].shape
            spec = pl.BlockSpec((shape[0] // 2, shape[1]), lambda i: (i, 0))
            given = [n for n, v in enumerate(values) if v is not None]
            made = (inward is not None) + (across is not None)

            def body(edge_ref, *refs):
                full = [None] * 5
                for n, ref in zip(given, refs):
                    full[n] = ref
                turn_kernel(edge_ref, *full, *refs[len(given) :])

            res = pl.pallas_call(
                body,
                grid=(2,),
                in_specs=[pl.BlockSpec(memory_space=pltpu.SMEM)] + [spec] * len(given),
                out_specs=[spec] * made,
                out_shape=[jax.ShapeDtypeStruct(shape, BF)] * made,
                compiler_params=pltpu.CompilerParams(vmem_limit_bytes=LIMIT * MIB),
                cost_estimate=pl.CostEstimate(flops=0, bytes_accessed=int(14 * shape[0] * shape[1] * COST), transcendentals=0),
                name="turn",
            )(self.knob(), *[values[n] for n in given])
            self.leave(res[0])
            if inward:
                pair = res[0]
            if across:
                send = res[-1]
                across["part"] = send
        self.across = inward
        if inward:
            inward["part"] = pair
            self.there = lax.ppermute(pair, "tp", [(1, 2), (2, 1)])
        self.inward, self.outward = job, across
        if job or across:
            perm = ([(0, 1), (3, 2)] if job else []) + ([(1, 0), (2, 3)] if across else [])
            self.got = lax.ppermute(send if across else fresh, "tp", perm)
        return job

    def take(self, job):
        while not job["done"]:
            self.tick()
        return job["got"], job["part"]


def group_sum(v, fsdp):
    v = v + lax.ppermute(v, "ctx", swap(2, 1))
    step = 1
    while step < fsdp:
        v = v + lax.ppermute(v, "fsdp", swap(fsdp, step))
        step *= 2
    return v


def per_device(
    sizes,
    inputs,
    lengths,
    cotangent,
    norm_gains,
    norm_shifts,
    qkv_weight,
    qv_bias,
    out_weight,
    out_bias,
    up_weight,
    up_bias,
    down_weight,
    down_bias,
):
    fsdp, tp = sizes
    clips, rows, width = inputs.shape
    assert clips == 1
    local = qkv_weight.shape[-1]
    units = up_weight.shape[-1]
    heads = local // HEAD_DIM
    wide = heads * LANES
    square = 4 * local
    lined = up_to(local, LANES)
    layers = norm_gains.shape[0]
    last = layers - 1
    me = lax.axis_index("ctx")
    full = up_to(rows, BACK)
    count = full // CHUNK
    each = range(count)
    unit = 256 if units % 256 == 0 else LANES
    tiles = units // unit
    length = lengths[0]
    flow = Flow(tp)

    spread = np.zeros((lined, wide), np.float32)
    for f in range(local):
        spread[f, f // HEAD_DIM * LANES + f % HEAD_DIM] = 1.0
    spread_line = jnp.asarray(spread, BF)
    spread_own = jnp.asarray(spread[:local], BF)
    gather_line = jnp.asarray(spread.T, BF)
    gather_own = jnp.asarray(spread[:local].T, BF)
    head_lane = np.arange(wide) % LANES
    q_extra = jnp.asarray((head_lane == HEAD_DIM)[None, :], F32)
    k_ones = jnp.asarray(((head_lane > HEAD_DIM) & (head_lane <= HEAD_DIM + 3))[None, :], F32)
    v_ones = jnp.asarray(((head_lane >= HEAD_DIM) & (head_lane <= HEAD_DIM + 1))[None, :], F32)
    row = jnp.arange(full)[:, None]
    live = (row < rows) & (row + me * rows < length)
    k_extra = (k_ones + jnp.where(live, 0.0, NEG) * q_extra).astype(BF)

    half = qkv_weight.shape[1] // 2

    def mine(w):
        return lax.dynamic_slice_in_dim(w, me * half, half, axis=0)

    def fetch(w):
        return lax.all_gather(w, ("fsdp", "ctx"), axis=0, tiled=True)

    attn_w, up_w, down_w = [], [], []
    for layer in range(layers):
        q3 = mine(qkv_weight[layer]).reshape(half, 3 * local)
        mats = [jnp.concatenate([mine(out_weight[layer]), q3], axis=1), mine(up_weight[layer]), mine(down_weight[layer])]
        if layer == 0:
            attn = fetch(mats[0])
            feeds = fetch(jnp.concatenate(mats[1:], axis=1))
            starts = (0, 0, units)
            held = (attn, feeds, feeds)
        else:
            everything = fetch(jnp.concatenate(mats, axis=1))
            starts = (0, square, square + units)
            held = (everything,) * 3
        attn_w.append(held[0])
        up_w.append((held[1], starts[1] // unit))
        down_w.append((held[2], starts[2] // unit))

    edge_spec = pl.BlockSpec(memory_space=pltpu.SMEM)

    def whole(a):
        return (a, block(a.shape, (0,) * a.ndim))

    me_flag = me.astype(jnp.int32)[None]
    ready = {}

    def give(layer, names, g, first_half=False):
        g = g.reshape(fsdp, 2, half, g.shape[1])
        if first_half:
            got = lax.ppermute(lax.dynamic_index_in_dim(g, 1 - me, 1, False), "ctx", swap(2, 1))
            mine_half = lax.dynamic_index_in_dim(g, me, 1, False) + got
            part = lax.psum_scatter(mine_half.reshape(fsdp * half, -1), "fsdp", scatter_dimension=0, tiled=True)
        else:
            part = lax.psum_scatter(g.reshape(fsdp * 2 * half, -1), ("fsdp", "ctx"), scatter_dimension=0, tiled=True)

        def finish():
            mine_half = flow.enter(part)[None, None]
            other = lax.ppermute(part, "ctx", swap(2, 1))[None, None]
            attn = len(names) == 2
            shapes = [(layers, 2 * half, local), (layers, 3, 2 * half, local)] if attn else [(layers, 2 * half, units)]
            outs = [(ready.get(n), shape, F32, block((1, *shape[1:]), (layer,) + (0,) * (len(shape) - 1)))
                    for n, shape in zip(names, shapes)]
            res = call(functools.partial(finish_kernel, local if attn else None), "finish", (1,),
                       [(me_flag, edge_spec), whole(mine_half), whole(other)], outs, moved=12 * part.size)
            ready.update(zip(names, res))
            flow.leave(res[0])

        return finish

    tall = ((0, full - rows), (0, 0))
    first_input = jnp.pad(inputs[0], tall)
    first_grad = jnp.where(live, jnp.pad(cotangent[0], tall), jnp.zeros((), BF))
    def rows_of(c, cols):
        return block((CHUNK, cols), (c, 0))

    def line(v):
        return (v[None, :], block((1, v.shape[0]), (0, 0)))

    def unit_line(v):
        return (v[None, :], pl.BlockSpec((1, unit), lambda t: (0, t)))

    def unit_cols(w):
        array, first = w
        return (array, pl.BlockSpec((array.shape[0], unit), lambda t: (0, first + t)))

    broad = max(width, square, units)
    sum_out = (None, (8, broad), F32, block((8, broad), (0, 0)))
    r_out = (None, (CHUNK, LANES), F32, block((CHUNK, LANES), (0, 0)))
    x_out = (None, (CHUNK, width), BF, block((CHUNK, width), (0, 0)))
    rows_out = (None, (CHUNK, width), F32, block((CHUNK, width), (0, 0)))
    wide_out = (None, (CHUNK, wide), BF, block((CHUNK, wide), (0, 0)))
    part_out = (None, (CHUNK, width), BF, block((CHUNK, width), (0, 0)))
    f32_rows = pltpu.VMEM((CHUNK, width), F32)
    bf_rows = pltpu.VMEM((CHUNK, width), BF)

    keep = [{n: [None] * count for n in ("hidden", "mid", "mid_grad", "slope", "q", "x1", "r1", "x2", "r2")}
            for _ in range(layers)]
    for k in keep:
        k["sums"] = jnp.zeros((8, broad), F32)
    grads = [None] * count

    def chunk(a):
        return (a, block(a.shape, (0, 0)))

    def given_grad(layer, c):
        return (first_grad, rows_of(c, width)) if layer == last else chunk(grads[c])

    def edge():
        return (flow.knob(), edge_spec)

    def both_of(job):
        spec = block((CHUNK, width), (0, 0))
        got, part = flow.take(job)
        return [(got, spec), (part, spec)]

    def out(store, name, cols, dtype, c):
        return (store.get(name) if c else None, (full, cols), dtype, rows_of(c, cols))

    def tile_out(store, name, c):
        return (store.get(name) if c else None, (full, units), BF, pl.BlockSpec((CHUNK, unit), lambda t: (c, t)))

    def project(layer, c, job):
        k = keep[layer]
        if job is None:
            pair = [(jnp.zeros((8, LANES), BF), block((8, LANES), (0, 0)))] * 2
            base, add = (first_input, rows_of(c, width)), jnp.zeros((width,), F32)
        else:
            pair = both_of(job)
            base, add = chunk(keep[layer - 1]["mid"][c]), down_bias[layer - 1]
        qb, vb = qv_bias[layer, 0], qv_bias[layer, 1]
        bias = jnp.concatenate([jnp.zeros_like(qb), qb, jnp.zeros_like(qb), vb])
        ins = [edge(), *pair, base, line(add), line(norm_gains[layer, 0]), line(norm_shifts[layer, 0]),
               (attn_w[layer], block((width, square), (0, 0))), line(bias), whole(spread_own), (k_extra, rows_of(c, wide)), whole(q_extra), whole(v_ones)]
        outs = [rows_out, x_out, r_out, out(k, "normed", width, BF, c), wide_out,
                (k.get("kv0") if c else None, (2, full, wide), BF, block((2, CHUNK, wide), (0, c, 0)))]
        res = call(functools.partial(project_kernel, job is None, local), "project", (1,), ins, outs,
                   flops=2 * CHUNK * width * square, moved=2 * width * square)
        k["hidden"][c], k["x1"][c], k["r1"][c], k["normed"], k["q"][c], k["kv0"] = res
        flow.leave(res[4])

    def share(layer):
        k = keep[layer]
        k["kv1"] = lax.ppermute(k["kv0"], "ctx", swap(2, 1))

    def head_specs(c, rows=CHUNK):
        q = pl.BlockSpec((rows, LANES), lambda h: (c, h))
        keys = pl.BlockSpec((1, full, LANES), lambda h: (0, 0, h))
        values = pl.BlockSpec((1, full, LANES), lambda h: (1, 0, h))
        return q, keys, values

    def attend(layer, c):
        k = keep[layer]
        q, keys, values = head_specs(c)
        ins = [edge(), (k["q"][c], pl.BlockSpec((CHUNK, LANES), lambda h: (0, h))), (k["kv0"], keys), (k["kv0"], values), (k["kv1"], keys), (k["kv1"], values),
               (gather_line, pl.BlockSpec((LANES, lined), lambda h: (h, 0))),
               (attn_w[layer], block((width, lined), (0, 0)))]
        outs = [(k.get("o") if c else None, (full, wide), BF, q), (k.get("qa") if c else None, (full, wide), BF, q),
                out(k, "attended", lined, BF, c), part_out]
        res = call(functools.partial(attend_kernel, heads), "attend", (heads,), ins, outs,
                   [pltpu.VMEM((CHUNK, lined), F32)], flops=8 * CHUNK * full * wide, moved=8 * full * wide)
        k["o"], k["qa"], k["attended"], part = res
        flow.leave(part)
        return flow.tick(part)

    def feed(layer, c, job):
        k = keep[layer]
        back = layer == last
        pair = both_of(job)
        ins = [edge(), *pair, chunk(k["hidden"][c]), line(out_bias[layer]), line(norm_gains[layer, 1]),
               line(norm_shifts[layer, 1]), unit_cols(up_w[layer]), unit_line(up_bias[layer]), unit_cols(down_w[layer])]
        outs = [rows_out, x_out, r_out, out(k, "normed2", width, BF, c), tile_out(k, "active", c)]
        scratch = [bf_rows, f32_rows]
        if back:
            ins += [given_grad(layer, c), whole(k["sums"])]
            outs += [out(k, "low", width, BF, c), tile_out(k, "d_upper", c), part_out, part_out, sum_out]
            scratch += [bf_rows, f32_rows]
        else:
            outs += [(None, (CHUNK, units), BF, pl.BlockSpec((CHUNK, unit), lambda t: (0, t))), part_out]
        res = call(functools.partial(feed_kernel, back, tiles), "feed", (tiles,), ins, outs, scratch,
                   flops=4 * CHUNK * width * units, moved=4 * width * units)
        k["mid"][c], k["x2"][c], k["r2"][c], k["normed2"], k["active"] = res[:5]
        if back:
            k["low"], k["d_upper"], late[c], part_back, k["sums"] = res[5:]
            flow.leave(part_back)
            return flow.tick(part_back)
        k["slope"][c], part = res[5:]
        flow.leave(part)
        return flow.tick(part)

    def norm2_back(layer, c, job):
        k = keep[layer]
        pair = both_of(job)
        ins = [edge(), *pair, given_grad(layer, c), chunk(k["x2"][c]), chunk(k["r2"][c]), line(norm_gains[layer, 1]),
               (attn_w[layer], block((width, lined), (0, 0))), whole(spread_line), whole(k["sums"])]
        outs = [rows_out, out(k, "low2", width, BF, c), out(k, "do", wide, BF, c), sum_out]
        k["mid_grad"][c], k["low2"], k["do"], k["sums"] = call(norm2_back_kernel, "norm2_back", (1,), ins, outs,
                                                    flops=2 * CHUNK * width * lined, moved=20 * CHUNK * width)
        flow.leave(k["do"])

    def attend_back(layer, c, sums):
        k = keep[layer]
        q, keys, values = head_specs(c, BACK)
        acc = pl.BlockSpec((full, LANES), lambda h: (0, h))
        first, done = sums is None, (c + 1) * BACK == full
        ins = [edge(), (k["qa"], q), (k["o"], q), (k["do"], q), (k["kv0"], keys), (k["kv0"], values), (k["kv1"], keys),
               (k["kv1"], values)]
        olds = [] if first else [(v, acc) for v in sums]
        old_dq = k.get("dq")
        everything = ins + olds + ([] if old_dq is None else [(old_dq, pl.BlockSpec(memory_space=pl.ANY))])
        aliases = {} if first else {len(ins) + n: 1 + n for n in range(2 if done else 4)}
        if old_dq is not None:
            aliases[len(everything) - 1] = 0
        kept = len(ins) + len(olds)
        sum_shape = jax.ShapeDtypeStruct((full, wide), F32)

        def body(*refs):
            attend_back_kernel(first, done, *refs[:kept], *refs[len(everything) :])

        res = pl.pallas_call(
            body,
            grid=(heads,),
            in_specs=[v for _, v in everything],
            out_specs=[q, acc, acc] + ([pl.BlockSpec((2, full, LANES), lambda h: (0, 0, h))] if done else [acc, acc]),
            out_shape=[jax.ShapeDtypeStruct((full, wide), BF), sum_shape, sum_shape]
            + ([jax.ShapeDtypeStruct((2, full, wide), BF)] if done else [sum_shape, sum_shape]),
            input_output_aliases=aliases,
            compiler_params=pltpu.CompilerParams(vmem_limit_bytes=LIMIT * MIB),
            cost_estimate=pl.CostEstimate(flops=int(20 * BACK * full * wide * COST), bytes_accessed=int(40 * full * wide * COST), transcendentals=0),
            name="attend_back",
        )(*[v for v, _ in everything])
        k["dq"] = res[0]
        flow.leave(res[0])
        return res[1:]

    def share_back(sums):
        dk0, dv0, theirs = sums
        return dk0, dv0, lax.ppermute(theirs, "ctx", swap(2, 1))

    def project_back(layer, c, shared):
        k = keep[layer]
        dk0, dv0, got = shared
        ins = [edge(), (k["dq"], rows_of(c, wide)), (dk0, rows_of(c, wide)), (dv0, rows_of(c, wide)),
               (got, block((2, CHUNK, wide), (0, c, 0))), whole(gather_own), (attn_w[layer], block((width, square), (0, 0))),
               whole(k["sums"])]
        outs = [out(k, "d_mixed", square, BF, c), part_out, sum_out]
        k["d_mixed"], part, k["sums"] = call(functools.partial(project_back_kernel, local), "project_back", (1,), ins, outs,
                                     flops=2 * CHUNK * width * square, moved=2 * width * square)
        flow.leave(part)
        return flow.tick(part)

    def norm1_back(layer, c, job):
        k = keep[layer]
        pair = both_of(job)
        ins = [edge(), *pair, chunk(k["mid_grad"][c]), chunk(k["x1"][c]), chunk(k["r1"][c]),
               line(norm_gains[layer, 0]), whole(k["sums"])]
        outs = [(k.get("grad"), (rows, 1, width), F32, block((CHUNK, 1, width), (c, 0, 0))), sum_out]
        k["grad"], k["sums"] = call(norm1_back_kernel, "norm1_back", (1,), ins, outs, moved=20 * CHUNK * width)
        flow.leave(k["sums"])

    def finish_output(layer, c, job):
        k = keep[layer]
        pair = both_of(job)
        ins = [edge(), *pair, chunk(k["mid"][c]), line(down_bias[layer])]
        (k["outputs"],) = call(output_kernel, "output", (1,), ins, [out(k, "outputs", width, BF, c)], moved=10 * CHUNK * width)
        flow.leave(k["outputs"])

    def feed_back(layer, c, job):
        k, b = keep[layer], keep[layer - 1]
        pair = both_of(job)
        ins = [edge(), *pair, chunk(k["mid_grad"][c]), chunk(k["x1"][c]), chunk(k["r1"][c]), line(norm_gains[layer, 0]),
               unit_cols(down_w[layer - 1]), unit_cols(up_w[layer - 1]),
               (b["slope"][c], pl.BlockSpec((CHUNK, unit), lambda t: (0, t))), whole(k["sums"]), whole(b["sums"])]
        outs = [rows_out, out(b, "low", width, BF, c), tile_out(b, "d_upper", c), part_out, sum_out, sum_out]
        res = call(functools.partial(feed_back_kernel, tiles), "feed_back", (tiles,), ins, outs, [bf_rows, f32_rows],
                   flops=4 * CHUNK * width * units, moved=4 * width * units)
        grads[c], b["low"], b["d_upper"], part, k["sums"], b["sums"] = res
        flow.leave(part)
        return flow.tick(part)

    def weight_grad(left, right):
        g = lax.dot_general(left, right, (((0,), (0,)), ((), ())), preferred_element_type=F32).astype(BF)
        return with_layout_constraint(g, Layout((0, 1)))

    def grad_down(layer):
        k = keep[layer]
        g = weight_grad(flow.enter(k["low"]), k["active"])
        flow.leave(g)
        return give(layer, ("down",), g)

    def grad_up(layer):
        k = keep[layer]
        g = weight_grad(flow.enter(k["normed2"]), k["d_upper"])
        flow.leave(g)
        return give(layer, ("up",), g)

    def grad_attn(layer):
        k = keep[layer]
        g2 = weight_grad(flow.enter(k["low2"]), k["attended"])
        g1 = weight_grad(k["normed"], k["d_mixed"])
        g = jnp.concatenate([g2[:, :local], g1[:, local:]], axis=1)
        flow.leave(g)
        return give(layer, ("out", "qkv"), g, layer == 0)

    jobs, late = [None] * count, [None] * count
    for layer in range(layers):
        for c in each:
            project(layer, c, jobs[c])
        share(layer)
        jobs = [attend(layer, c) for c in each]
        jobs = [feed(layer, c, jobs[c]) for c in each]
    late_jobs, endings = [None] * count, []
    for layer in reversed(range(layers)):
        k = keep[layer]
        sums = None
        for c in each:
            norm2_back(layer, c, jobs[c])
            if c == 0:
                endings.append(grad_down(layer))
            if c == 1:
                endings.append(grad_up(layer))
            final = (c + 1) * CHUNK % BACK == 0
            if c < count - 1:
                late_jobs[c] = flow.tick(late[c]) if layer == last else flow.tick()
            if final:
                sums = attend_back(layer, c * CHUNK // BACK, sums)
        if layer == last:
            late_jobs[-1] = flow.tick(late[-1])
        shared = share_back(sums)
        for c in each:
            jobs[c] = project_back(layer, c, shared)
            if layer == last:
                finish_output(layer, c, late_jobs[c])
            elif endings and c < len(endings) - 2:
                endings[c]()
        endings.append(grad_attn(layer))
        for c in each:
            if layer > 0:
                jobs[c] = feed_back(layer, c, jobs[c])
            else:
                norm1_back(layer, c, jobs[c])
    group = group_sum(jnp.concatenate([flow.enter(keep[0]["sums"])] + [k["sums"] for k in keep[1:]]), fsdp)
    for ending in endings[-3:]:
        ending()

    def all_of(*shape):
        return (None, shape, F32, block(shape, (0,) * len(shape)))

    gains, shifts, qv, out_b, up_b, down_b = call(
        functools.partial(vectors_kernel, layers, local), "vectors", (1,), [whole(group)],
        [all_of(layers, 2, width)] * 2 + [all_of(layers, 2, local), all_of(layers, width), all_of(layers, units), all_of(layers, width)],
    )
    return (
        keep[last]["outputs"][None, :rows],
        keep[0]["grad"].reshape(1, rows, width),
        gains,
        shifts,
        ready["qkv"].transpose(0, 2, 1, 3),
        qv,
        ready["out"],
        out_b,
        ready["up"],
        up_b,
        ready["down"],
        down_b,
    )


def solution(mesh):
    in_specs = (
        P("fsdp", "ctx", None),
        P("fsdp"),
        P("fsdp", "ctx", None),
        P(),
        P(),
        P(None, "fsdp", None, "tp"),
        P(None, None, "tp"),
        P(None, "fsdp", "tp"),
        P(),
        P(None, "fsdp", "tp"),
        P(None, "tp"),
        P(None, "fsdp", "tp"),
        P(),
    )
    out_specs = (
        P("fsdp", "ctx", None),
        P("fsdp", "ctx", None),
        P(),
        P(),
        P(None, "fsdp", None, "tp"),
        P(None, None, "tp"),
        P(None, "fsdp", "tp"),
        P(),
        P(None, "fsdp", "tp"),
        P(None, "tp"),
        P(None, "fsdp", "tp"),
        P(),
    )
    sizes = (mesh.shape["fsdp"], mesh.shape["tp"])
    return jax.shard_map(
        functools.partial(per_device, sizes), mesh=mesh, in_specs=in_specs, out_specs=out_specs, check_vma=False
    )
```

```python
import functools

import jax
import jax.numpy as jnp
import numpy as np
from jax import lax
from jax.experimental import pallas as pl
from jax.experimental.layout import Layout, with_layout_constraint
from jax.experimental.pallas import tpu as pltpu
from jax.sharding import PartitionSpec as P

HEAD_DIM = 80
LANES = 128
CHUNK = 192
BACK = 384
EPSILON = 1e-05
NEG = -1e30
SCALE = HEAD_DIM**-0.5
SCALE2 = SCALE * float(np.log2(np.e))
BF = jnp.bfloat16
F32 = jnp.float32
NT = (((1,), (1,)), ((), ()))
NN = (((1,), (0,)), ((), ()))
MIB = 1024 * 1024
LIMIT = 20
COST = 0.1


def mm(a, b, dims=NN):
    return lax.dot_general(a, b, dims, preferred_element_type=F32)


def up_to(n, m):
    return -(-n // m) * m


def block(shape, index):
    return pl.BlockSpec(shape, lambda *grid: index)


def call(kernel, name, grid, ins, outs, scratch=(), flops=0, moved=0, limit=LIMIT):
    olds = [(n, o[0]) for n, o in enumerate(outs) if o[0] is not None]
    specs = [spec for _, spec in ins] + [pl.BlockSpec(memory_space=pl.ANY)] * len(olds)
    live = len(ins)

    def body(*refs):
        kernel(*refs[:live], *refs[live + len(olds) :])

    return pl.pallas_call(
        body,
        grid=grid,
        in_specs=specs,
        out_specs=[o[3] for o in outs],
        out_shape=[jax.ShapeDtypeStruct(o[1], o[2]) for o in outs],
        scratch_shapes=list(scratch),
        input_output_aliases={live + k: n for k, (n, _) in enumerate(olds)},
        compiler_params=pltpu.CompilerParams(vmem_limit_bytes=limit * MIB),
        cost_estimate=pl.CostEstimate(flops=int(flops * COST), bytes_accessed=int(moved * COST), transcendentals=0),
        name=name,
    )(*[a for a, _ in ins], *[o for _, o in olds])


def lane_iota(shape):
    return lax.broadcasted_iota(jnp.int32, shape, 1)


def norm_stats(v):
    center = jnp.mean(v, axis=-1, keepdims=True)
    centred = v - center
    spread = jnp.mean(centred * centred, axis=-1, keepdims=True)
    r = lax.rsqrt(spread + EPSILON)
    return centred * r, r


def norm_back(x_ref, r_ref, gain, dn):
    xhat, r = x_ref[...].astype(F32), r_ref[:, :1]
    dx = dn * gain
    back = r * (dx - jnp.mean(dx, axis=-1, keepdims=True) - xhat * jnp.mean(dx * xhat, axis=-1, keepdims=True))
    return back, dn * xhat


def gelu_pair(u):
    cdf = 0.5 * (1.0 + lax.erf(u * float(np.sqrt(0.5))))
    pdf = jnp.exp(-0.5 * u * u) * float(1.0 / np.sqrt(2 * np.pi))
    return u * cdf, cdf + u * pdf


def summed(edge_ref, got_ref, part_ref):
    return jnp.where(edge_ref[0] == 1, got_ref[...], part_ref[...]).astype(F32)


def rows_sum(v):
    return jnp.sum(v, axis=0, keepdims=True)


def keep_norm(xhat, r, x_ref, r_ref):
    x_ref[...] = xhat.astype(BF)
    r_ref[...] = jnp.broadcast_to(r, r_ref.shape)


def add_sums(ref, at, *values):
    for n, v in enumerate(values):
        ref[at + n : at + n + 1, : v.shape[1]] += v


NORM1_ROW, NORM2_ROW, OUT_ROW, DOWN_ROW, MIXED_ROW, UP_ROW = 0, 2, 4, 5, 6, 7


def add_unit_sums(ref, tile, d):
    n = d.shape[1]
    ref[UP_ROW : UP_ROW + 1, pl.ds(pl.multiple_of(tile * n, n), n)] += rows_sum(d.astype(F32))


def project_kernel(
    first, local, edge_ref, got_ref, part_ref, base_ref, add_ref, gain_ref, shift_ref, w_ref, bias_ref, spread_ref,
    ke_ref, qe_ref, ve_ref, h_ref, x_ref, r_ref, n_ref, q_ref, kv_ref,
):
    h = base_ref[...].astype(F32)
    if not first:
        h = h + summed(edge_ref, got_ref, part_ref) + add_ref[...]
    h_ref[...] = h
    xhat, r = norm_stats(h)
    keep_norm(xhat, r, x_ref, r_ref)
    n = (xhat * gain_ref[...] + shift_ref[...]).astype(BF)
    n_ref[...] = n
    m = (mm(n, w_ref[...]) + bias_ref[...]).astype(BF)
    spread = spread_ref[...]
    q_ref[...] = (mm(m[:, local : 2 * local], spread) + qe_ref[...]).astype(BF)
    kv_ref[0] = (mm(m[:, 2 * local : 3 * local], spread) + ke_ref[...].astype(F32)).astype(BF)
    kv_ref[1] = (mm(m[:, 3 * local :], spread) + ve_ref[...]).astype(BF)


def split3(v):
    hi = v.astype(BF).astype(F32)
    mid = (v - hi).astype(BF).astype(F32)
    return hi, mid, v - hi - mid


def attend_kernel(
    heads, edge_ref, q_ref, k0_ref, v0_ref, k1_ref, v1_ref, gather_ref, w_ref, o_ref, qa_ref, att_ref, part_ref, acc_ref
):
    q = q_ref[...]
    s0 = mm(q, k0_ref[0], NT)
    s1 = mm(q, k1_ref[0], NT)
    top = jnp.maximum(jnp.max(s0, axis=1, keepdims=True), jnp.max(s1, axis=1, keepdims=True))
    p0 = jnp.exp2((s0 - top) * SCALE2).astype(BF)
    p1 = jnp.exp2((s1 - top) * SCALE2).astype(BF)
    o = mm(p0, v0_ref[0]) + mm(p1, v1_ref[0])
    lane = lane_iota(o.shape)
    total = jnp.sum(jnp.where(lane == HEAD_DIM, o, 0.0), axis=1, keepdims=True)
    o = jnp.where(lane < HEAD_DIM, o / total, 0.0).astype(BF)
    o_ref[...] = o
    hi, mid, lo = split3(-(top + jnp.log2(total) * (1.0 / SCALE2)))
    qa = jnp.where(lane == HEAD_DIM + 1, hi, q.astype(F32))
    qa = jnp.where(lane == HEAD_DIM + 2, mid, qa)
    qa = jnp.where(lane == HEAD_DIM + 3, lo, qa)
    qa_ref[...] = qa.astype(BF)
    head = pl.program_id(0)
    here = mm(o, gather_ref[...])

    @pl.when(head == 0)
    def _():
        acc_ref[...] = here

    @pl.when(head > 0)
    def _():
        acc_ref[...] += here

    @pl.when(head == heads - 1)
    def _():
        att = acc_ref[...].astype(BF)
        att_ref[...] = att
        part_ref[...] = mm(att, w_ref[...], NT).astype(BF)


def feed_kernel(
    back, tiles, edge_ref, got_ref, part_ref, h_ref, add_ref, gain_ref, shift_ref, up_ref, bias_ref, down_ref, *refs
):
    if back:
        (g_ref, old_ref, mid_ref, x_ref, r_ref, n_ref, act_ref, low_ref, d_ref, out_ref, back_ref, sum_ref,
         n_s, acc_s, low_s, acc2_s) = refs
    else:
        mid_ref, x_ref, r_ref, n_ref, act_ref, slope_ref, out_ref, n_s, acc_s = refs
    tile = pl.program_id(0)

    @pl.when(tile == 0)
    def _():
        mid = h_ref[...] + summed(edge_ref, got_ref, part_ref) + add_ref[...]
        mid_ref[...] = mid
        xhat, r = norm_stats(mid)
        keep_norm(xhat, r, x_ref, r_ref)
        n = (xhat * gain_ref[...] + shift_ref[...]).astype(BF)
        n_ref[...] = n
        n_s[...] = n
        if back:
            low = g_ref[...]
            low_ref[...] = low
            low_s[...] = low
            sum_ref[...] = old_ref[...]
            add_sums(sum_ref, DOWN_ROW, rows_sum(low.astype(F32)))

    act, slope = gelu_pair(mm(n_s[...], up_ref[...]) + bias_ref[...])
    act = act.astype(BF)
    act_ref[...] = act
    here = mm(act, down_ref[...], NT)
    if back:
        d = (mm(low_s[...], down_ref[...]) * slope).astype(BF)
        d_ref[...] = d
        add_unit_sums(sum_ref, tile, d)
        here2 = mm(d, up_ref[...], NT)
    else:
        slope_ref[...] = slope.astype(BF)

    @pl.when(tile == 0)
    def _():
        acc_s[...] = here
        if back:
            acc2_s[...] = here2

    @pl.when(tile > 0)
    def _():
        acc_s[...] += here
        if back:
            acc2_s[...] += here2

    @pl.when(tile == tiles - 1)
    def _():
        out_ref[...] = acc_s[...].astype(BF)
        if back:
            back_ref[...] = acc2_s[...].astype(BF)


def norm2_back_kernel(
    edge_ref, got_ref, part_ref, g_ref, x_ref, r_ref, gain_ref, w_ref, spread_ref, old_ref, mg_ref, low_ref, do_ref, sum_ref
):
    dn = summed(edge_ref, got_ref, part_ref)
    back, gg = norm_back(x_ref, r_ref, gain_ref[...], dn)
    mg = g_ref[...].astype(F32) + back
    mg_ref[...] = mg
    low = mg.astype(BF)
    low_ref[...] = low
    do_ref[...] = mm(mm(low, w_ref[...]).astype(BF), spread_ref[...]).astype(BF)
    sum_ref[...] = old_ref[...]
    add_sums(sum_ref, NORM2_ROW, rows_sum(gg), rows_sum(dn), rows_sum(mg))


def attend_back_kernel(first, done, edge_ref, qa_ref, o_ref, do_ref, k0_ref, v0_ref, k1_ref, v1_ref, *refs):
    olds = (None,) * 4 if first else refs[:4]
    dq_ref, dk0_ref, dv0_ref, *rest = refs[len(refs) - (4 if done else 5) :]
    dk1_ref, dv1_ref = (None, None) if done else rest
    qa = qa_ref[...]
    do = do_ref[...].astype(F32)
    lane = lane_iota(do.shape)
    delta = -jnp.sum(o_ref[...].astype(F32) * do, axis=1, keepdims=True)
    hi = delta.astype(BF).astype(F32)
    doa = jnp.where(lane == HEAD_DIM, hi, do)
    doa = jnp.where(lane == HEAD_DIM + 1, delta - hi, doa).astype(BF)
    dqt = None
    for k_ref, v_ref, dk_ref, dv_ref, dk_old, dv_old in (
        (k0_ref, v0_ref, dk0_ref, dv0_ref, olds[0], olds[1]),
        (k1_ref, v1_ref, dk1_ref, dv1_ref, olds[2], olds[3]),
    ):
        k = k_ref[0]
        pt = jnp.exp2(mm(k, qa, NT) * SCALE2)
        dst = (pt * mm(v_ref[0], doa, NT)).astype(BF)
        dv = mm(pt.astype(BF), doa)
        dk = mm(dst, qa)
        if not first:
            dv, dk = dv_old[...] + dv, dk_old[...] + dk
        if dk_ref is None:
            rest[0][0] = (dk * SCALE).astype(BF)
            rest[0][1] = dv.astype(BF)
        else:
            dk_ref[...] = dk
            dv_ref[...] = dv
        part = mm(k.T, dst)
        dqt = part if dqt is None else dqt + part
    dq_ref[...] = (dqt.T * SCALE).astype(BF)


def project_back_kernel(
    local, edge_ref, dq_ref, dk_ref, dv_ref, got_ref, gather_ref, w_ref, old_ref, d_ref, part_ref, sum_ref
):
    gather = gather_ref[...]
    dq = mm(dq_ref[...], gather).astype(BF)
    dk = mm((dk_ref[...] * SCALE + got_ref[0].astype(F32)).astype(BF), gather).astype(BF)
    dv = mm((dv_ref[...] + got_ref[1].astype(F32)).astype(BF), gather).astype(BF)
    d = jnp.concatenate([jnp.zeros_like(dq), dq, dk, dv], axis=1)
    d_ref[...] = d
    part_ref[...] = mm(d, w_ref[...], NT).astype(BF)
    sum_ref[...] = old_ref[...]
    add_sums(sum_ref, MIXED_ROW, rows_sum(d.astype(F32)))


def norm1_back_kernel(edge_ref, got_ref, part_ref, mg_ref, x_ref, r_ref, gain_ref, old_ref, g_ref, sum_ref):
    dn = summed(edge_ref, got_ref, part_ref)
    back, gg = norm_back(x_ref, r_ref, gain_ref[...], dn)
    g_ref[...] = (mg_ref[...] + back).reshape(g_ref.shape)
    sum_ref[...] = old_ref[...]
    add_sums(sum_ref, NORM1_ROW, rows_sum(gg), rows_sum(dn))


def output_kernel(edge_ref, got_ref, part_ref, mid_ref, add_ref, out_ref):
    out_ref[...] = (mid_ref[...] + summed(edge_ref, got_ref, part_ref) + add_ref[...]).astype(BF)


def vectors_kernel(layers, local, sum_ref, gain_ref, shift_ref, qv_ref, out_ref, up_ref, down_ref):
    for n in range(layers):
        def row(at, start, size):
            return sum_ref[8 * n + at : 8 * n + at + 1, :][:, start : start + size]

        width = gain_ref.shape[2]
        for at, first in ((0, NORM1_ROW), (1, NORM2_ROW)):
            gain_ref[n, at : at + 1, :] = row(first, 0, width)
            shift_ref[n, at : at + 1, :] = row(first + 1, 0, width)
        qv_ref[n, 0:1, :] = row(MIXED_ROW, local, local)
        qv_ref[n, 1:2, :] = row(MIXED_ROW, 3 * local, local)
        out_ref[n : n + 1, :] = row(OUT_ROW, 0, width)
        up_ref[n : n + 1, :] = row(UP_ROW, 0, up_ref.shape[1])
        down_ref[n : n + 1, :] = row(DOWN_ROW, 0, width)


def finish_kernel(cuts, me_ref, own_ref, other_ref, *out_refs):
    half = own_ref.shape[2]
    first = me_ref[0] == 0
    for m in range(own_ref.shape[1]):
        for at, (a, b) in ((0, (own_ref, other_ref)), (half, (other_ref, own_ref))):
            v = jnp.where(first, a[0, m].astype(F32), b[0, m].astype(F32))
            if cuts is None:
                out_refs[m][0, at : at + half, :] = v
            else:
                out_refs[0][0, at : at + half, :] = v[:, :cuts]
                for t in range(3):
                    out_refs[1][0, t, at : at + half, :] = v[:, (t + 1) * cuts : (t + 2) * cuts]


def feed_back_kernel(
    tiles, edge_ref, got_ref, part_ref, mg_ref, x_ref, r_ref, gain_ref, down_ref, up_ref, slope_ref, old_ref, lold_ref,
    g_ref, low_ref, d_ref, out_ref, sum_ref, lsum_ref, low_s, acc_s,
):
    tile = pl.program_id(0)

    @pl.when(tile == 0)
    def _():
        dn = summed(edge_ref, got_ref, part_ref)
        back, gg = norm_back(x_ref, r_ref, gain_ref[...], dn)
        g = mg_ref[...] + back
        g_ref[...] = g
        low = g.astype(BF)
        low_ref[...] = low
        low_s[...] = low
        sum_ref[...] = old_ref[...]
        lsum_ref[...] = lold_ref[...]
        add_sums(sum_ref, NORM1_ROW, rows_sum(gg), rows_sum(dn))
        add_sums(lsum_ref, DOWN_ROW, rows_sum(g))

    d = (mm(low_s[...], down_ref[...]) * slope_ref[...].astype(F32)).astype(BF)
    d_ref[...] = d
    add_unit_sums(lsum_ref, tile, d)
    here = mm(d, up_ref[...], NT)

    @pl.when(tile == 0)
    def _():
        acc_s[...] = here

    @pl.when(tile > 0)
    def _():
        acc_s[...] += here

    @pl.when(tile == tiles - 1)
    def _():
        out_ref[...] = acc_s[...].astype(BF)


def swap(n, step):
    return [(i, i ^ step) for i in range(n)]


def turn_kernel(edge_ref, *refs):
    part, got, pair, there, fresh = refs[:5]
    outs = refs[5:]
    if part is not None:
        outs[0][...] = part[...] + got[...]
    if pair is not None:
        total = pair[...] + there[...]
        outs[-1][...] = total if fresh is None else jnp.where(edge_ref[0] == 1, fresh[...], total)


class Flow:
    def __init__(self, tp):
        self.tp, self.token = tp, None
        self.inward = self.across = self.outward = None
        index = lax.axis_index("tp")
        self.edge = jnp.where((index == 0) | (index == 3), 1, 0).astype(jnp.int32)[None]

    def enter(self, value):
        if self.token is not None:
            value, self.token = lax.optimization_barrier((value, self.token))
        return value

    def leave(self, value):
        self.token = value

    def knob(self):
        return self.enter(self.edge)

    def tick(self, fresh=None):
        if self.tp != 4:
            whole = lax.psum(fresh, "tp")
            return {"part": whole, "got": whole, "done": True}
        inward, across, outward = self.inward, self.across, self.outward
        got = self.got if inward or outward else None
        if outward:
            outward.update(got=got, done=True)
        job = {"part": fresh, "done": False} if fresh is not None else None
        pair = send = None
        if inward or across:
            values = [inward and inward["part"], inward and got, across and across["part"], across and self.there,
                      fresh if across else None]
            shape = (inward or across)["part"].shape
            spec = pl.BlockSpec((shape[0] // 2, shape[1]), lambda i: (i, 0))
            given = [n for n, v in enumerate(values) if v is not None]
            made = (inward is not None) + (across is not None)

            def body(edge_ref, *refs):
                full = [None] * 5
                for n, ref in zip(given, refs):
                    full[n] = ref
                turn_kernel(edge_ref, *full, *refs[len(given) :])

            res = pl.pallas_call(
                body,
                grid=(2,),
                in_specs=[pl.BlockSpec(memory_space=pltpu.SMEM)] + [spec] * len(given),
                out_specs=[spec] * made,
                out_shape=[jax.ShapeDtypeStruct(shape, BF)] * made,
                compiler_params=pltpu.CompilerParams(vmem_limit_bytes=LIMIT * MIB),
                cost_estimate=pl.CostEstimate(flops=0, bytes_accessed=int(14 * shape[0] * shape[1] * COST), transcendentals=0),
                name="turn",
            )(self.knob(), *[values[n] for n in given])
            self.leave(res[0])
            if inward:
                pair = res[0]
            if across:
                send = res[-1]
                across["part"] = send
        self.across = inward
        if inward:
            inward["part"] = pair
            self.there = lax.ppermute(pair, "tp", [(1, 2), (2, 1)])
        self.inward, self.outward = job, across
        if job or across:
            perm = ([(0, 1), (3, 2)] if job else []) + ([(1, 0), (2, 3)] if across else [])
            self.got = lax.ppermute(send if across else fresh, "tp", perm)
        return job

    def take(self, job):
        while not job["done"]:
            self.tick()
        return job["got"], job["part"]


def group_sum(v, fsdp):
    v = v + lax.ppermute(v, "ctx", swap(2, 1))
    step = 1
    while step < fsdp:
        v = v + lax.ppermute(v, "fsdp", swap(fsdp, step))
        step *= 2
    return v


def per_device(
    sizes,
    inputs,
    lengths,
    cotangent,
    norm_gains,
    norm_shifts,
    qkv_weight,
    qv_bias,
    out_weight,
    out_bias,
    up_weight,
    up_bias,
    down_weight,
    down_bias,
):
    fsdp, tp = sizes
    clips, rows, width = inputs.shape
    assert clips == 1
    local = qkv_weight.shape[-1]
    units = up_weight.shape[-1]
    heads = local // HEAD_DIM
    wide = heads * LANES
    square = 4 * local
    lined = up_to(local, LANES)
    layers = norm_gains.shape[0]
    last = layers - 1
    me = lax.axis_index("ctx")
    full = up_to(rows, BACK)
    count = full // CHUNK
    each = range(count)
    unit = 256 if units % 256 == 0 else LANES
    tiles = units // unit
    length = lengths[0]
    flow = Flow(tp)

    spread = np.zeros((lined, wide), np.float32)
    for f in range(local):
        spread[f, f // HEAD_DIM * LANES + f % HEAD_DIM] = 1.0
    spread_line = jnp.asarray(spread, BF)
    spread_own = jnp.asarray(spread[:local], BF)
    gather_line = jnp.asarray(spread.T, BF)
    gather_own = jnp.asarray(spread[:local].T, BF)
    head_lane = np.arange(wide) % LANES
    q_extra = jnp.asarray((head_lane == HEAD_DIM)[None, :], F32)
    k_ones = jnp.asarray(((head_lane > HEAD_DIM) & (head_lane <= HEAD_DIM + 3))[None, :], F32)
    v_ones = jnp.asarray(((head_lane >= HEAD_DIM) & (head_lane <= HEAD_DIM + 1))[None, :], F32)
    row = jnp.arange(full)[:, None]
    live = (row < rows) & (row + me * rows < length)
    k_extra = (k_ones + jnp.where(live, 0.0, NEG) * q_extra).astype(BF)

    half = qkv_weight.shape[1] // 2

    def mine(w):
        return lax.dynamic_slice_in_dim(w, me * half, half, axis=0)

    def fetch(w):
        return lax.all_gather(w, ("fsdp", "ctx"), axis=0, tiled=True)

    attn_w, up_w, down_w = [], [], []
    for layer in range(layers):
        q3 = mine(qkv_weight[layer]).reshape(half, 3 * local)
        mats = [jnp.concatenate([mine(out_weight[layer]), q3], axis=1), mine(up_weight[layer]), mine(down_weight[layer])]
        if layer == 0:
            attn = fetch(mats[0])
            feeds = fetch(jnp.concatenate(mats[1:], axis=1))
            starts = (0, 0, units)
            held = (attn, feeds, feeds)
        else:
            everything = fetch(jnp.concatenate(mats, axis=1))
            starts = (0, square, square + units)
            held = (everything,) * 3
        attn_w.append(held[0])
        up_w.append((held[1], starts[1] // unit))
        down_w.append((held[2], starts[2] // unit))

    edge_spec = pl.BlockSpec(memory_space=pltpu.SMEM)

    def whole(a):
        return (a, block(a.shape, (0,) * a.ndim))

    me_flag = me.astype(jnp.int32)[None]
    ready = {}

    def give(layer, names, g, first_half=False):
        g = g.reshape(fsdp, 2, half, g.shape[1])
        if first_half:
            got = lax.ppermute(lax.dynamic_index_in_dim(g, 1 - me, 1, False), "ctx", swap(2, 1))
            mine_half = lax.dynamic_index_in_dim(g, me, 1, False) + got
            part = lax.psum_scatter(mine_half.reshape(fsdp * half, -1), "fsdp", scatter_dimension=0, tiled=True)
        else:
            part = lax.psum_scatter(g.reshape(fsdp * 2 * half, -1), ("fsdp", "ctx"), scatter_dimension=0, tiled=True)

        def finish():
            mine_half = flow.enter(part)[None, None]
            other = lax.ppermute(part, "ctx", swap(2, 1))[None, None]
            attn = len(names) == 2
            shapes = [(layers, 2 * half, local), (layers, 3, 2 * half, local)] if attn else [(layers, 2 * half, units)]
            outs = [(ready.get(n), shape, F32, block((1, *shape[1:]), (layer,) + (0,) * (len(shape) - 1)))
                    for n, shape in zip(names, shapes)]
            res = call(functools.partial(finish_kernel, local if attn else None), "finish", (1,),
                       [(me_flag, edge_spec), whole(mine_half), whole(other)], outs, moved=12 * part.size)
            ready.update(zip(names, res))
            flow.leave(res[0])

        return finish

    tall = ((0, full - rows), (0, 0))
    first_input = jnp.pad(inputs[0], tall)
    first_grad = jnp.where(live, jnp.pad(cotangent[0], tall), jnp.zeros((), BF))
    def rows_of(c, cols):
        return block((CHUNK, cols), (c, 0))

    def line(v):
        return (v[None, :], block((1, v.shape[0]), (0, 0)))

    def unit_line(v):
        return (v[None, :], pl.BlockSpec((1, unit), lambda t: (0, t)))

    def unit_cols(w):
        array, first = w
        return (array, pl.BlockSpec((array.shape[0], unit), lambda t: (0, first + t)))

    broad = max(width, square, units)
    sum_out = (None, (8, broad), F32, block((8, broad), (0, 0)))
    r_out = (None, (CHUNK, LANES), F32, block((CHUNK, LANES), (0, 0)))
    x_out = (None, (CHUNK, width), BF, block((CHUNK, width), (0, 0)))
    rows_out = (None, (CHUNK, width), F32, block((CHUNK, width), (0, 0)))
    wide_out = (None, (CHUNK, wide), BF, block((CHUNK, wide), (0, 0)))
    part_out = (None, (CHUNK, width), BF, block((CHUNK, width), (0, 0)))
    f32_rows = pltpu.VMEM((CHUNK, width), F32)
    bf_rows = pltpu.VMEM((CHUNK, width), BF)

    keep = [{n: [None] * count for n in ("hidden", "mid", "mid_grad", "slope", "q", "x1", "r1", "x2", "r2")}
            for _ in range(layers)]
    for k in keep:
        k["sums"] = jnp.zeros((8, broad), F32)
    grads = [None] * count

    def chunk(a):
        return (a, block(a.shape, (0, 0)))

    def given_grad(layer, c):
        return (first_grad, rows_of(c, width)) if layer == last else chunk(grads[c])

    def edge():
        return (flow.knob(), edge_spec)

    def both_of(job):
        spec = block((CHUNK, width), (0, 0))
        got, part = flow.take(job)
        return [(got, spec), (part, spec)]

    def out(store, name, cols, dtype, c):
        return (store.get(name) if c else None, (full, cols), dtype, rows_of(c, cols))

    def tile_out(store, name, c):
        return (store.get(name) if c else None, (full, units), BF, pl.BlockSpec((CHUNK, unit), lambda t: (c, t)))

    def project(layer, c, job):
        k = keep[layer]
        if job is None:
            pair = [(jnp.zeros((8, LANES), BF), block((8, LANES), (0, 0)))] * 2
            base, add = (first_input, rows_of(c, width)), jnp.zeros((width,), F32)
        else:
            pair = both_of(job)
            base, add = chunk(keep[layer - 1]["mid"][c]), down_bias[layer - 1]
        qb, vb = qv_bias[layer, 0], qv_bias[layer, 1]
        bias = jnp.concatenate([jnp.zeros_like(qb), qb, jnp.zeros_like(qb), vb])
        ins = [edge(), *pair, base, line(add), line(norm_gains[layer, 0]), line(norm_shifts[layer, 0]),
               (attn_w[layer], block((width, square), (0, 0))), line(bias), whole(spread_own), (k_extra, rows_of(c, wide)), whole(q_extra), whole(v_ones)]
        outs = [rows_out, x_out, r_out, out(k, "normed", width, BF, c), wide_out,
                (k.get("kv0") if c else None, (2, full, wide), BF, block((2, CHUNK, wide), (0, c, 0)))]
        res = call(functools.partial(project_kernel, job is None, local), "project", (1,), ins, outs,
                   flops=2 * CHUNK * width * square, moved=2 * width * square)
        k["hidden"][c], k["x1"][c], k["r1"][c], k["normed"], k["q"][c], k["kv0"] = res
        flow.leave(res[4])

    def share(layer):
        k = keep[layer]
        k["kv1"] = lax.ppermute(k["kv0"], "ctx", swap(2, 1))

    def head_specs(c, rows=CHUNK):
        q = pl.BlockSpec((rows, LANES), lambda h: (c, h))
        keys = pl.BlockSpec((1, full, LANES), lambda h: (0, 0, h))
        values = pl.BlockSpec((1, full, LANES), lambda h: (1, 0, h))
        return q, keys, values

    def attend(layer, c):
        k = keep[layer]
        q, keys, values = head_specs(c)
        ins = [edge(), (k["q"][c], pl.BlockSpec((CHUNK, LANES), lambda h: (0, h))), (k["kv0"], keys), (k["kv0"], values), (k["kv1"], keys), (k["kv1"], values),
               (gather_line, pl.BlockSpec((LANES, lined), lambda h: (h, 0))),
               (attn_w[layer], block((width, lined), (0, 0)))]
        outs = [(k.get("o") if c else None, (full, wide), BF, q), (k.get("qa") if c else None, (full, wide), BF, q),
                out(k, "attended", lined, BF, c), part_out]
        res = call(functools.partial(attend_kernel, heads), "attend", (heads,), ins, outs,
                   [pltpu.VMEM((CHUNK, lined), F32)], flops=8 * CHUNK * full * wide, moved=8 * full * wide)
        k["o"], k["qa"], k["attended"], part = res
        flow.leave(part)
        return flow.tick(part)

    def feed(layer, c, job):
        k = keep[layer]
        back = layer == last
        pair = both_of(job)
        ins = [edge(), *pair, chunk(k["hidden"][c]), line(out_bias[layer]), line(norm_gains[layer, 1]),
               line(norm_shifts[layer, 1]), unit_cols(up_w[layer]), unit_line(up_bias[layer]), unit_cols(down_w[layer])]
        outs = [rows_out, x_out, r_out, out(k, "normed2", width, BF, c), tile_out(k, "active", c)]
        scratch = [bf_rows, f32_rows]
        if back:
            ins += [given_grad(layer, c), whole(k["sums"])]
            outs += [out(k, "low", width, BF, c), tile_out(k, "d_upper", c), part_out, part_out, sum_out]
            scratch += [bf_rows, f32_rows]
        else:
            outs += [(None, (CHUNK, units), BF, pl.BlockSpec((CHUNK, unit), lambda t: (0, t))), part_out]
        res = call(functools.partial(feed_kernel, back, tiles), "feed", (tiles,), ins, outs, scratch,
                   flops=4 * CHUNK * width * units, moved=4 * width * units)
        k["mid"][c], k["x2"][c], k["r2"][c], k["normed2"], k["active"] = res[:5]
        if back:
            k["low"], k["d_upper"], late[c], part_back, k["sums"] = res[5:]
            flow.leave(part_back)
            return flow.tick(part_back)
        k["slope"][c], part = res[5:]
        flow.leave(part)
        return flow.tick(part)

    def norm2_back(layer, c, job):
        k = keep[layer]
        pair = both_of(job)
        ins = [edge(), *pair, given_grad(layer, c), chunk(k["x2"][c]), chunk(k["r2"][c]), line(norm_gains[layer, 1]),
               (attn_w[layer], block((width, lined), (0, 0))), whole(spread_line), whole(k["sums"])]
        outs = [rows_out, out(k, "low2", width, BF, c), out(k, "do", wide, BF, c), sum_out]
        k["mid_grad"][c], k["low2"], k["do"], k["sums"] = call(norm2_back_kernel, "norm2_back", (1,), ins, outs,
                                                    flops=2 * CHUNK * width * lined, moved=20 * CHUNK * width)
        flow.leave(k["do"])

    def attend_back(layer, c, sums):
        k = keep[layer]
        q, keys, values = head_specs(c, BACK)
        acc = pl.BlockSpec((full, LANES), lambda h: (0, h))
        first, done = sums is None, (c + 1) * BACK == full
        ins = [edge(), (k["qa"], q), (k["o"], q), (k["do"], q), (k["kv0"], keys), (k["kv0"], values), (k["kv1"], keys),
               (k["kv1"], values)]
        olds = [] if first else [(v, acc) for v in sums]
        old_dq = k.get("dq")
        everything = ins + olds + ([] if old_dq is None else [(old_dq, pl.BlockSpec(memory_space=pl.ANY))])
        aliases = {} if first else {len(ins) + n: 1 + n for n in range(2 if done else 4)}
        if old_dq is not None:
            aliases[len(everything) - 1] = 0
        kept = len(ins) + len(olds)
        sum_shape = jax.ShapeDtypeStruct((full, wide), F32)

        def body(*refs):
            attend_back_kernel(first, done, *refs[:kept], *refs[len(everything) :])

        res = pl.pallas_call(
            body,
            grid=(heads,),
            in_specs=[v for _, v in everything],
            out_specs=[q, acc, acc] + ([pl.BlockSpec((2, full, LANES), lambda h: (0, 0, h))] if done else [acc, acc]),
            out_shape=[jax.ShapeDtypeStruct((full, wide), BF), sum_shape, sum_shape]
            + ([jax.ShapeDtypeStruct((2, full, wide), BF)] if done else [sum_shape, sum_shape]),
            input_output_aliases=aliases,
            compiler_params=pltpu.CompilerParams(vmem_limit_bytes=LIMIT * MIB),
            cost_estimate=pl.CostEstimate(flops=int(20 * BACK * full * wide * COST), bytes_accessed=int(40 * full * wide * COST), transcendentals=0),
            name="attend_back",
        )(*[v for v, _ in everything])
        k["dq"] = res[0]
        flow.leave(res[0])
        return res[1:]

    def share_back(sums):
        dk0, dv0, theirs = sums
        return dk0, dv0, lax.ppermute(theirs, "ctx", swap(2, 1))

    def project_back(layer, c, shared):
        k = keep[layer]
        dk0, dv0, got = shared
        ins = [edge(), (k["dq"], rows_of(c, wide)), (dk0, rows_of(c, wide)), (dv0, rows_of(c, wide)),
               (got, block((2, CHUNK, wide), (0, c, 0))), whole(gather_own), (attn_w[layer], block((width, square), (0, 0))),
               whole(k["sums"])]
        outs = [out(k, "d_mixed", square, BF, c), part_out, sum_out]
        k["d_mixed"], part, k["sums"] = call(functools.partial(project_back_kernel, local), "project_back", (1,), ins, outs,
                                     flops=2 * CHUNK * width * square, moved=2 * width * square)
        flow.leave(part)
        return flow.tick(part)

    def norm1_back(layer, c, job):
        k = keep[layer]
        pair = both_of(job)
        ins = [edge(), *pair, chunk(k["mid_grad"][c]), chunk(k["x1"][c]), chunk(k["r1"][c]),
               line(norm_gains[layer, 0]), whole(k["sums"])]
        outs = [(k.get("grad"), (rows, 1, width), F32, block((CHUNK, 1, width), (c, 0, 0))), sum_out]
        k["grad"], k["sums"] = call(norm1_back_kernel, "norm1_back", (1,), ins, outs, moved=20 * CHUNK * width)
        flow.leave(k["sums"])

    def finish_output(layer, c, job):
        k = keep[layer]
        pair = both_of(job)
        ins = [edge(), *pair, chunk(k["mid"][c]), line(down_bias[layer])]
        (k["outputs"],) = call(output_kernel, "output", (1,), ins, [out(k, "outputs", width, BF, c)], moved=10 * CHUNK * width)
        flow.leave(k["outputs"])

    def feed_back(layer, c, job):
        k, b = keep[layer], keep[layer - 1]
        pair = both_of(job)
        ins = [edge(), *pair, chunk(k["mid_grad"][c]), chunk(k["x1"][c]), chunk(k["r1"][c]), line(norm_gains[layer, 0]),
               unit_cols(down_w[layer - 1]), unit_cols(up_w[layer - 1]),
               (b["slope"][c], pl.BlockSpec((CHUNK, unit), lambda t: (0, t))), whole(k["sums"]), whole(b["sums"])]
        outs = [rows_out, out(b, "low", width, BF, c), tile_out(b, "d_upper", c), part_out, sum_out, sum_out]
        res = call(functools.partial(feed_back_kernel, tiles), "feed_back", (tiles,), ins, outs, [bf_rows, f32_rows],
                   flops=4 * CHUNK * width * units, moved=4 * width * units)
        grads[c], b["low"], b["d_upper"], part, k["sums"], b["sums"] = res
        flow.leave(part)
        return flow.tick(part)

    def weight_grad(left, right):
        g = lax.dot_general(left, right, (((0,), (0,)), ((), ())), preferred_element_type=F32).astype(BF)
        return with_layout_constraint(g, Layout((0, 1)))

    def grad_down(layer):
        k = keep[layer]
        g = weight_grad(flow.enter(k["low"]), k["active"])
        flow.leave(g)
        return give(layer, ("down",), g)

    def grad_up(layer):
        k = keep[layer]
        g = weight_grad(flow.enter(k["normed2"]), k["d_upper"])
        flow.leave(g)
        return give(layer, ("up",), g)

    def grad_attn(layer):
        k = keep[layer]
        g2 = weight_grad(flow.enter(k["low2"]), k["attended"])
        g1 = weight_grad(k["normed"], k["d_mixed"])
        g = jnp.concatenate([g2[:, :local], g1[:, local:]], axis=1)
        flow.leave(g)
        return give(layer, ("out", "qkv"), g, layer == 0)

    jobs, late = [None] * count, [None] * count
    for layer in range(layers):
        for c in each:
            project(layer, c, jobs[c])
        share(layer)
        jobs = [attend(layer, c) for c in each]
        jobs = [feed(layer, c, jobs[c]) for c in each]
    late_jobs, endings = [None] * count, []
    for layer in reversed(range(layers)):
        k = keep[layer]
        sums = None
        for c in each:
            norm2_back(layer, c, jobs[c])
            if c == 0:
                endings.append(grad_down(layer))
            if c == 1:
                endings.append(grad_up(layer))
            final = (c + 1) * CHUNK % BACK == 0
            if c < count - 1:
                if layer == last:
                    late_jobs[c] = flow.tick(late[c])
                elif layer == last - 1 and c == 0:
                    late_jobs[-1] = flow.tick(late[-1])
                else:
                    flow.tick()
            if final:
                sums = attend_back(layer, c * CHUNK // BACK, sums)
        shared = share_back(sums)
        for c in each:
            jobs[c] = project_back(layer, c, shared)
            if layer == last and c < count - 1:
                finish_output(layer, c, late_jobs[c])
            if layer == last - 1 and c == 0:
                finish_output(last, count - 1, late_jobs[-1])
            if layer < last and endings and c < len(endings) - 2:
                endings[c]()
        endings.append(grad_attn(layer))
        for c in each:
            if layer > 0:
                jobs[c] = feed_back(layer, c, jobs[c])
            else:
                norm1_back(layer, c, jobs[c])
    group = group_sum(jnp.concatenate([flow.enter(keep[0]["sums"])] + [k["sums"] for k in keep[1:]]), fsdp)
    for ending in endings[-3:]:
        ending()

    def all_of(*shape):
        return (None, shape, F32, block(shape, (0,) * len(shape)))

    gains, shifts, qv, out_b, up_b, down_b = call(
        functools.partial(vectors_kernel, layers, local), "vectors", (1,), [whole(group)],
        [all_of(layers, 2, width)] * 2 + [all_of(layers, 2, local), all_of(layers, width), all_of(layers, units), all_of(layers, width)],
    )
    return (
        keep[last]["outputs"][None, :rows],
        keep[0]["grad"].reshape(1, rows, width),
        gains,
        shifts,
        ready["qkv"].transpose(0, 2, 1, 3),
        qv,
        ready["out"],
        out_b,
        ready["up"],
        up_b,
        ready["down"],
        down_b,
    )


def solution(mesh):
    in_specs = (
        P("fsdp", "ctx", None),
        P("fsdp"),
        P("fsdp", "ctx", None),
        P(),
        P(),
        P(None, "fsdp", None, "tp"),
        P(None, None, "tp"),
        P(None, "fsdp", "tp"),
        P(),
        P(None, "fsdp", "tp"),
        P(None, "tp"),
        P(None, "fsdp", "tp"),
        P(),
    )
    out_specs = (
        P("fsdp", "ctx", None),
        P("fsdp", "ctx", None),
        P(),
        P(),
        P(None, "fsdp", None, "tp"),
        P(None, None, "tp"),
        P(None, "fsdp", "tp"),
        P(),
        P(None, "fsdp", "tp"),
        P(None, "tp"),
        P(None, "fsdp", "tp"),
        P(),
    )
    sizes = (mesh.shape["fsdp"], mesh.shape["tp"])
    return jax.shard_map(
        functools.partial(per_device, sizes), mesh=mesh, in_specs=in_specs, out_specs=out_specs, check_vma=False
    )
```
